32 devices in a mesh: groups: 2 (over y), req: 4 (over z), mp: 4 (over x, core).
Axes of the slice: x: 2, y: 2, z: 4, core: 2. Of those that a mesh axis runs over, the one named last changes fastest.
Arguments:
- tokens: bfloat16 [3072, 4096], P(('groups', 'req'), 'mp'), parts along dimension 0, may hold values from -6 to 6
- lengths: int32 [8, 128], P(('groups', 'req')), parts along dimension 0, may hold values from 1 to 4, 384 in all within a row
- adapter_holder_index: int32 [1024, 1], P(('groups', 'req')), parts along dimension 0, may hold values from 0 to 3; in each aligned block of 128 rows (0 to 127, 128 to 255, ...) at most 33 rows name the same one
- adapter_place_index: int32 [1024], P(('groups', 'req')), parts along dimension 0, may hold values from 0 to 4
- value_weight: bfloat16 [4096, 1024], P(None, 'mp'), may hold values from -0.09375 to 0.09375
- adapter_down_weight: bfloat16 [4096, 20, 64], P('mp', 'req'), may hold values from -0.09375 to 0.09375
- adapter_up_weight: bfloat16 [20, 64, 1024], P('req', None, 'mp'), may hold values from -0.75 to 0.75
Outputs:
- values_out: bfloat16 [3072, 1024], P(('groups', 'req'), 'mp'), parts along dimension 0
The draws below stay inside these ranges and needn't reach their ends.
There are 2 independent parts, one for each index of `groups`. The reference program is written for one: setup_inputs(seed, part) draws one part's arguments, and reference() takes and returns one part's arrays. A program takes and returns all parts, laid end to end along the dimension named above; an argument that names none is the same for every part. Nothing has to cross between parts.
Inputs may be any that keep to these rules, and one draw needn't show every extreme that they name: `adapter_holder_index`: in each aligned block of 128 rows (the prompts of one index of req) no value appears more than 33 times, a bound that some block reaches. `lengths`: each row sums to 384.
All inputs are finite; a program needn't handle non-finite values.
Results may differ from the reference program's by a relative error of at most 0.0043.
Values may be sent and summed in bfloat16 or wider, within the bound.
A program may use at most 64 MiB of HBM per device.

```python
import math
import jax
import jax.numpy as jnp
import numpy as np
from jax import lax

MODEL_WIDTH = 4096
VALUE_WIDTH = 1024
ADAPTER_RANK = 64
ADP_DEV = 5
LMAX = 4
TOK_DEV = 384
REQ_DEV = 128
MOSTREQ = 33
ADAPTER_TOTAL = 20
REQUESTS = 512
TOKENS = 1536
N_REQ = 4


def with_ends(array, stream_key, least, largest):
    place = [jax.random.randint(jax.random.fold_in(stream_key, axis), (), 0, length) for axis, length in enumerate(array.shape)]
    main_axis = array.shape.index(max(array.shape))
    neighbour = place[:main_axis] + [(place[main_axis] + 1) % array.shape[main_axis]] + place[main_axis + 1:]
    return array.at[tuple(place)].set(least).at[tuple(neighbour)].set(largest)


def shard_levels(stream_key, extent, split, low, largest):
    def one(dim, shards_of):
        heights = jax.random.uniform(jax.random.fold_in(jax.random.fold_in(stream_key, 6), dim), (shards_of,), jnp.float32, low / len(split), largest / len(split))
        return jnp.repeat(jnp.exp(heights), extent[dim] // shards_of).reshape((-1,) + (1,) * (len(extent) - dim - 1))

    gain = one(*split[0])
    for cut in split[1:]:
        gain = gain * one(*cut)
    return gain


def length_profile(count, total, reach, slope):
    portions = [(1 << 20) // math.isqrt(grade ** slope) + 1 for grade in range(2, count + 1)]
    rest, holding = total - reach - (count - 1), [1] * (count - 1)
    while rest > 0:
        movable = [i for i in range(count - 1) if holding[i] < reach]
        pool, budget = sum([portions[i] for i in movable]), rest
        for i in movable:
            addition = min(reach - holding[i], max(1, budget * portions[i] // pool), rest)
            holding[i] = holding[i] + addition
            rest = rest - addition
    return np.array([reach] + holding)


def ragged_sizes(stream_key, count, total, limit, lean):
    if count == 2:
        one = jax.random.randint(stream_key, (), max(1, total - limit), min(limit, total - 1) + 1)
        return jnp.stack([one, total - one])
    sizes = jnp.asarray(length_profile(count, total, limit, lean), jnp.int32)
    pairs = (count - 1) // 2
    giver, sink = sizes[1:1 + 2 * pairs:2], sizes[2:2 + 2 * pairs:2]
    slack = jnp.minimum(giver - 1, limit - sink)
    shifted = jax.random.randint(jax.random.fold_in(stream_key, 1), (pairs,), 0, 1 << 20) % (slack + 1)
    sizes = sizes.at[1:1 + 2 * pairs:2].set(giver - shifted).at[2:2 + 2 * pairs:2].set(sink + shifted)
    return sizes[jax.random.permutation(jax.random.fold_in(stream_key, 2), count)]


def routed_block(stream_key, own, number, rows, number_of, top, bound, slope):
    order = jax.random.permutation(stream_key, number_of)
    heavy_load, ordinary = portions_of(number_of, rows * top, bound, slope, True), portions_of(number_of, rows * top, bound, slope, False)
    places = jnp.arange(number_of)

    def named(sizes, offset_by):
        used = int((sizes > 0).sum())
        fixed = max(1, used // 4)
        passed = fixed + (places - fixed + offset_by * (used - fixed)) % max(1, number_of - fixed)
        return jnp.zeros((number_of,), jnp.int32).at[order[jnp.where(places < fixed, places, passed)]].set(jnp.asarray(sizes, jnp.int32))

    sizes = jnp.where(number % 4 == 0, named(heavy_load, number // 4), named(ordinary, number - number // 4 - 1))
    mixed = jax.random.permutation(jax.random.fold_in(own, 3), number_of)
    donor, taker = mixed[0:number_of // 2 * 2:2], mixed[1:number_of // 2 * 2:2]
    slack = jnp.minimum(sizes[donor] - 1, bound - sizes[taker]) // 2
    slack = jnp.where((donor == order[0]) | (taker == order[0]) | (sizes[taker] == 0), 0, jnp.maximum(slack, 0))
    passed = jax.random.randint(jax.random.fold_in(own, 4), (number_of // 2,), 0, 1 << 20) % (slack + 1)
    sizes = sizes.at[donor].add(-passed).at[taker].add(passed)
    items = jnp.searchsorted(jnp.cumsum(sizes), jnp.arange(rows * top), side="right").astype(jnp.int32)
    table = items.reshape(top, rows).T
    table = table[jax.random.permutation(jax.random.fold_in(own, 1), rows)]
    offset_by = jax.random.randint(jax.random.fold_in(own, 2), (rows, 1), 0, top)
    return jnp.take_along_axis(table, (jnp.arange(top)[None, :] + offset_by) % top, axis=1)


def portions_of(count, total, bound, lean, full):
    weights = [(1 << 20) // math.isqrt(grade ** lean) + 1 for grade in range(1, count + 1)]
    largest = bound if full else min(bound, max(-(-total // count), total * weights[0] // sum(weights)))
    least = 1 if total - largest >= count - 1 else 0
    counts, spare = [largest] + [least] * (count - 1), total - largest - least * (count - 1)
    while spare > 0:
        free = [i for i in range(1, count) if counts[i] < largest] or [i for i in range(1, count) if counts[i] < bound]
        pool, remaining = sum([weights[i] for i in free]), spare
        for i in free:
            more = min(bound - counts[i], max(1, remaining * weights[i] // pool), spare)
            counts[i] = counts[i] + more
            spare = spare - more
    return np.array(counts)


def scatter_about(own_key, extent, spread, limit, cuts=(), kind=jnp.bfloat16):
    drawn = spread * jax.random.normal(own_key, extent, jnp.float32)
    if cuts:
        drawn = drawn * shard_levels(own_key, extent, cuts, -0.22, 0.18)
    return jnp.clip(drawn, -limit, limit).astype(kind)


def setup_inputs(seed: int = 0, part: int = 0) -> dict:
    arg_keys = jax.random.split(jax.random.key(seed), 8)
    part_keys = jax.random.split(jax.random.fold_in(arg_keys[7], part), 8)
    tokens = scatter_about(part_keys[0], (TOKENS, MODEL_WIDTH), 1.0, 6.0, ((0, 4), (1, 4)))
    lengths = jax.vmap(lambda own: ragged_sizes(own, REQ_DEV, TOK_DEV, LMAX, 2))(jax.random.split(part_keys[1], N_REQ)).reshape((N_REQ, REQ_DEV)).astype(jnp.int32)
    adapter_holder_index_keys = jax.random.split(jax.random.fold_in(part_keys[2], 1), REQUESTS // REQ_DEV)
    adapter_holder_index_turns = jax.random.permutation(jax.random.fold_in(part_keys[2], 3), REQUESTS // REQ_DEV)
    adapter_holder_index = jax.vmap(lambda own, number: routed_block(jax.random.fold_in(part_keys[2], 2), own, number, REQ_DEV, N_REQ, 1, MOSTREQ, 2))(adapter_holder_index_keys, adapter_holder_index_turns).reshape((REQUESTS, 1))
    adapter_place_index = with_ends(jax.random.randint(part_keys[3], (REQUESTS,), 0, ADP_DEV), jax.random.fold_in(part_keys[3], 1), 0, ADP_DEV - 1).astype(jnp.int32)
    value_weight = scatter_about(arg_keys[4], (MODEL_WIDTH, VALUE_WIDTH), MODEL_WIDTH ** -0.5, 0.09375, ((1, 4),))
    adapter_down_weight = scatter_about(arg_keys[5], (MODEL_WIDTH, ADAPTER_TOTAL, ADAPTER_RANK), MODEL_WIDTH ** -0.5, 0.09375, ((0, 4), (1, 4)))
    adapter_up_weight = scatter_about(arg_keys[6], (ADAPTER_TOTAL, ADAPTER_RANK, VALUE_WIDTH), ADAPTER_RANK ** -0.5, 0.75, ((0, 4), (2, 4)))
    return dict(tokens=tokens, lengths=lengths, adapter_holder_index=adapter_holder_index, adapter_place_index=adapter_place_index, value_weight=value_weight, adapter_down_weight=adapter_down_weight, adapter_up_weight=adapter_up_weight)


def reference(tokens, lengths, adapter_holder_index, adapter_place_index, value_weight, adapter_down_weight, adapter_up_weight):
    adapter_ids = (adapter_holder_index[:, 0] * ADP_DEV + adapter_place_index).astype(jnp.int32).reshape(N_REQ, REQ_DEV)
    prompt_ends = jnp.cumsum(lengths, axis=1)
    position = jnp.arange(TOK_DEV, dtype=jnp.int32)
    request_of = jnp.sum((position[None, :, None] >= prompt_ends[:, None, :]).astype(jnp.int32), axis=2)
    token_adapter = jnp.take_along_axis(adapter_ids, request_of, axis=1).astype(jnp.int32)
    blocks = tokens.reshape(N_REQ, TOK_DEV, MODEL_WIDTH)

    def one_piece(item):
        piece_rows, piece_index_list = item
        down_factor_rows = adapter_down_weight[:, piece_index_list, :].astype(jnp.float32)
        reduced_rank_output = jnp.einsum('td,dtr->tr', piece_rows.astype(jnp.float32), down_factor_rows).astype(jnp.bfloat16)
        up_factor_rows = adapter_up_weight[piece_index_list].astype(jnp.float32)
        adapter_update = jnp.einsum('id,idz->iz', reduced_rank_output.astype(jnp.float32), up_factor_rows).astype(jnp.bfloat16)
        base_output = jnp.dot(piece_rows, value_weight, preferred_element_type=jnp.float32)
        return (base_output + 0.5 * adapter_update.astype(jnp.float32)).astype(jnp.bfloat16)

    def one_block(item):
        block_rows, block_ids = item
        pieces = (block_rows.reshape(8, TOK_DEV // 8, MODEL_WIDTH), block_ids.reshape(8, TOK_DEV // 8))
        return lax.map(one_piece, pieces).reshape(TOK_DEV, VALUE_WIDTH)

    produced = lax.map(one_block, (blocks, token_adapter))
    return produced.reshape(N_REQ * TOK_DEV, VALUE_WIDTH)
```

```python
import functools

import jax
import jax.numpy as jnp
from jax import lax
from jax.experimental import pallas as pl
from jax.experimental.pallas import tpu as pltpu
from jax.sharding import PartitionSpec as P

LMAX = 4
REQ_DEV = 128
GATHER_BYTES = 24 << 20

PIECES = 4
SLICES = 4
MESH = pl.DeviceIdType.MESH


def adapter_kernel(
    peers,
    held,
    rank,
    tok,
    lengths,
    holder,
    place,
    weight,
    down,
    up,
    out,
    tok_all,
    weight_here,
    down_all,
    up_all,
    low_all,
    base,
    low_sum,
    adapter_of,
    local_sem,
    z_send_sem,
    z_recv_sem,
    y_send_sem,
    y_recv_sem,
    x_send_sem,
    x_recv_sem,
    low_send_sem,
    low_recv_sem,
):
    rows, feats = tok.shape
    cols = out.shape[1]
    width = held * rank
    half = rows // 2
    piece = feats // (2 * PIECES)
    batch = rows // SLICES
    g, z, m = lax.axis_index("groups"), lax.axis_index("req"), lax.axis_index("mp")
    sibling = m + 1 - 2 * lax.rem(m, 2)
    across = lax.rem(m + 2, 4)
    diagonal = lax.rem(sibling + 2, 4)

    def remote(src, dst, send_sem, recv_sem, device):
        return pltpu.make_async_remote_copy(
            src_ref=src,
            dst_ref=dst,
            send_sem=send_sem,
            recv_sem=recv_sem,
            device_id=device,
            device_id_type=MESH,
        )

    def strip(h, side, c):
        if c < PIECES:
            lanes = pl.ds(pl.multiple_of(side * (feats // 2) + c * piece, 128), piece)
            return down_all.at[h, :, lanes]
        lanes = pl.ds(pl.multiple_of(side * (cols // 2), 128), cols // 2)
        return up_all.at[h, :, lanes]

    def own_strip(c):
        if c < PIECES:
            lanes = pl.ds(pl.multiple_of(g * (feats // 2) + c * piece, 128), piece)
            return down.at[:, lanes]
        lanes = pl.ds(pl.multiple_of(g * (cols // 2), 128), cols // 2)
        return up.at[:, lanes]

    def step_of(way):
        return 1 if way == 0 else -1

    def has(way, d):
        return z >= d if way == 0 else z + d <= peers - 1

    def has_next(way):
        return z + 1 <= peers - 1 if way == 0 else z >= 1

    def z_send(way, d, c):
        h = z - step_of(way) * d
        target = strip(h, g, c)
        return remote(
            own_strip(c) if d == 0 else target,
            target,
            z_send_sem.at[way, d, c],
            z_recv_sem.at[way, d, c],
            {"req": z + step_of(way)},
        )

    def z_recv(way, d, c):
        target = strip(z - step_of(way) * d, g, c)
        return remote(
            target,
            target,
            z_send_sem.at[way, d - 1, c],
            z_recv_sem.at[way, d - 1, c],
            {"req": z - step_of(way)},
        )

    def y_copy(way, d, c, side):
        target = strip(z - step_of(way) * d, side, c)
        return remote(
            target,
            target,
            y_send_sem.at[way, d - 1, c],
            y_recv_sem.at[way, d - 1, c],
            {"groups": 1 - g},
        )

    def pass_on(way, d, c):
        @pl.when(has(way, d))
        def _():
            z_recv(way, d, c).wait_recv()
            if d < peers - 1:
                pl.when(has_next(way))(z_send(way, d, c).start)
            y_copy(way, d, c, g).start()

    def batch_of(b, s):
        return tok_all.at[b, pl.ds(s * batch, batch)]

    def x_copy(kind, s):
        if kind == 2:
            src = batch_of(across, s)
        else:
            src = tok.at[pl.ds(s * batch, batch)]
        return remote(
            src,
            batch_of(across if kind == 2 else m, s),
            x_send_sem.at[kind, s],
            x_recv_sem.at[kind, s],
            {"mp": across if kind == 0 else sibling},
        )

    def x_recv(kind, s):
        target = batch_of((across, sibling, diagonal)[kind], s)
        return remote(
            target,
            target,
            x_send_sem.at[kind, s],
            x_recv_sem.at[kind, s],
            {"mp": across if kind == 0 else sibling},
        )

    def low_copy(i, b):
        return remote(
            low_all.at[m],
            low_all.at[m if b is None else b],
            low_send_sem.at[i],
            low_recv_sem.at[i],
            {"mp": (across, sibling, diagonal)[i]},
        )

    local = [
        pltpu.make_async_copy(tok, tok_all.at[m], local_sem.at[0]),
        pltpu.make_async_copy(down, down_all.at[z], local_sem.at[1]),
        pltpu.make_async_copy(weight, weight_here, local_sem.at[2]),
        pltpu.make_async_copy(up, up_all.at[z], local_sem.at[3]),
    ]
    for copy in local:
        copy.start()

    barrier = pltpu.get_barrier_semaphore()
    for device in ({"mp": across}, {"mp": sibling}, {"mp": diagonal}, {"groups": 1 - g}):
        pl.semaphore_signal(barrier, inc=1, device_id=device, device_id_type=MESH)
    for way in range(2):

        @pl.when(has_next(way))
        def _(way=way):
            pl.semaphore_signal(
                barrier, inc=1, device_id={"req": z + step_of(way)}, device_id_type=MESH
            )

    prompts = lengths.shape[1]
    lens = lengths[...]
    earlier = lax.broadcasted_iota(jnp.int32, (prompts, prompts), 0) <= lax.broadcasted_iota(
        jnp.int32, (prompts, prompts), 1
    )
    ends = jnp.dot(
        jnp.broadcast_to(lens, (8, prompts)).astype(jnp.float32).astype(jnp.bfloat16),
        earlier.astype(jnp.float32).astype(jnp.bfloat16),
        preferred_element_type=jnp.float32,
    )[0:1].astype(jnp.int32)
    position = lax.broadcasted_iota(jnp.int32, (rows, prompts), 0)
    inside = (position < ends) & (position >= ends - lens)
    named = jnp.where(inside, holder[...] * held + place[...], 0)
    adapter_of[...] = jnp.sum(named, axis=1, keepdims=True)

    beside = lax.div(z + peers - 1, peers) + lax.div(2 * peers - 2 - z, peers)
    pl.semaphore_wait(barrier, 4 + beside)

    for c in range(PIECES):
        for way in range(2):
            pl.when(has_next(way))(z_send(way, 0, c).start)
    for s in range(SLICES):
        x_copy(0, s).start()
    for s in range(SLICES):
        x_copy(1, s).start()

    def add_base(b, first=False):
        term = jnp.dot(
            tok_all[b],
            weight_here[pl.ds(pl.multiple_of(b * feats, 128), feats)],
            preferred_element_type=jnp.float32,
        )
        if first:
            base[...] = term
        else:
            base[...] += term

    lane = lax.broadcasted_iota(jnp.int32, (1, width), 1)

    def member(h, part):
        return adapter_of[part * half : (part + 1) * half, :] == lane // rank + h * held

    def fold(part, turned):
        shape = (2 * rank, width) if turned else (width, 2 * rank)
        one = lax.broadcasted_iota(jnp.int32, shape, 1 if turned else 0)
        two = lax.broadcasted_iota(jnp.int32, shape, 0 if turned else 1)
        return (lax.rem(one, rank) == two - part * rank).astype(jnp.float32).astype(jnp.bfloat16)

    def add_low(h, first=False):
        total = jnp.zeros((half, 2 * rank), jnp.float32)
        for part in range(2):
            partial = lax.dot_general(
                tok_all[m, part * half : (part + 1) * half],
                down_all[h],
                (((1,), (1,)), ((), ())),
                preferred_element_type=jnp.float32,
            )
            kept = jnp.where(member(h, part), partial, 0.0).astype(jnp.bfloat16)
            total += jnp.dot(kept, fold(part, False), preferred_element_type=jnp.float32)
        if first:
            low_sum[...] = total
        else:
            low_sum[...] += total

    def finish(way, d):
        @pl.when(has(way, d))
        def _():
            for c in range(PIECES):
                y_copy(way, d, c, 1 - g).wait_recv()
            add_low(z - step_of(way) * d)

    local[0].wait()
    local[1].wait()
    add_low(z, first=True)
    local[2].wait()
    add_base(m, first=True)
    slot = 0
    for d in range(1, peers):
        for c in range(PIECES):
            for way in range(2):
                pass_on(way, d, c)
            if slot < SLICES:
                x_recv(0, slot).wait_recv()
                x_copy(2, slot).start()
            slot += 1
        if d == 1:
            for s in range(SLICES):
                x_recv(1, s).wait_recv()
            add_base(sibling)
            add_base(across)
        if d == 2:
            for s in range(SLICES):
                x_recv(2, s).wait_recv()
            add_base(diagonal)
        if d >= 2:
            for way in range(2):
                finish(way, d - 1)
    for way in range(2):
        pl.when(has_next(way))(z_send(way, 0, PIECES).start)
    for way in range(2):
        finish(way, peers - 1)

    low_all[m] = low_sum[...].astype(jnp.bfloat16)
    for i in range(3):
        low_copy(i, None).start()
    for d in range(1, peers):
        for way in range(2):
            pass_on(way, d, PIECES)
    for i, b in enumerate((across, sibling, diagonal)):
        low_copy(i, b).wait_recv()
    local[3].wait()
    low = low_all[0].astype(jnp.float32)
    for b in range(1, 4):
        low += low_all[b].astype(jnp.float32)
    low = low.astype(jnp.bfloat16)
    for d in range(1, peers):
        for way in range(2):
            pl.when(has(way, d))(y_copy(way, d, PIECES, 1 - g).wait_recv)
    for part in range(2):
        spread = jnp.dot(low, fold(part, True), preferred_element_type=jnp.float32)
        term = jnp.zeros((half, cols), jnp.float32)
        for h in range(peers):
            kept = jnp.where(member(h, part), spread, 0.0).astype(jnp.bfloat16)
            term += jnp.dot(kept, up_all[h], preferred_element_type=jnp.float32)
        term = term.astype(jnp.bfloat16).astype(jnp.float32)
        here = pl.ds(part * half, half)
        out[here, :] = (base[here, :] + 0.5 * term).astype(jnp.bfloat16)

    for s in range(SLICES):
        for kind in range(3):
            x_copy(kind, s).wait_send()
    for i in range(3):
        low_copy(i, None).wait_send()
    for way in range(2):
        for c in range(PIECES + 1):
            for d in range(peers - 1):
                sent = has_next(way) if d == 0 else has_next(way) & has(way, d)
                pl.when(sent)(z_send(way, d, c).wait_send)
            for d in range(1, peers):
                pl.when(has(way, d))(y_copy(way, d, c, g).wait_send)


def grouped_update(token_rows, slot_ids, down_factor_sets, up_sets, reduce_fn):
    count = token_rows.shape[0] * token_rows.shape[1]
    flat_rows = token_rows.reshape(count, token_rows.shape[2])
    flat_ids = slot_ids.reshape(count)
    held = down_factor_sets.shape[0]
    blocks = (count + 127) // 128 + held
    grouped = blocks * 128
    valid = flat_ids >= 0
    member = (flat_ids[:, None] == jnp.arange(held, dtype=jnp.int32)[None, :]).astype(jnp.int32)
    group_sizes = jnp.sum(member, axis=0)
    padded = (group_sizes + 127) // 128 * 128
    group_end = jnp.cumsum(padded)
    group_start = group_end - padded
    within = jnp.sum(jnp.cumsum(member, axis=0) * member, axis=1) - 1
    target = jnp.where(valid, jnp.sum(member * group_start[None, :], axis=1) + within, grouped)
    source = (
        jnp.zeros((grouped,), jnp.int32)
        .at[target]
        .set(jnp.arange(count, dtype=jnp.int32), mode="drop")
    )
    filled = jnp.zeros((grouped,), jnp.bool_).at[target].set(True, mode="drop")
    grouped_rows = jnp.where(filled[:, None], flat_rows[source], jnp.zeros((), jnp.bfloat16))
    grouped_rows = grouped_rows.reshape(blocks, 128, flat_rows.shape[1])
    block_first = jnp.arange(blocks, dtype=jnp.int32) * 128
    block_adapter = jnp.minimum(
        jnp.sum((block_first[:, None] >= group_end[None, :]).astype(jnp.int32), axis=1), held - 1
    )
    partial_value = jnp.einsum(
        "bkf,bfr->bkr",
        grouped_rows,
        down_factor_sets[block_adapter],
        preferred_element_type=jnp.float32,
    )
    reduced_rank_output = reduce_fn(partial_value).astype(jnp.bfloat16)
    term = jnp.einsum(
        "bkr,brc->bkc",
        reduced_rank_output,
        up_sets[block_adapter],
        preferred_element_type=jnp.float32,
    )
    term = term.astype(jnp.bfloat16).reshape(grouped, up_sets.shape[2])
    picked = jnp.where(
        valid[:, None], term[jnp.minimum(target, grouped - 1)], jnp.zeros((), jnp.bfloat16)
    )
    return picked.reshape(token_rows.shape[0], token_rows.shape[1], up_sets.shape[2])


def body(
    tokens,
    lengths,
    adapter_holder_index,
    adapter_place_index,
    value_weight,
    adapter_down_weight,
    adapter_up_weight,
):
    tok_rows = tokens.shape[0]
    peers = lax.axis_size("req")
    request_cap = max(2, REQ_DEV // peers + 1)
    slots = request_cap * LMAX
    lengths_row = lengths[0]
    prompt_ends = jnp.cumsum(lengths_row)
    prompt_starts = prompt_ends - lengths_row
    owners = adapter_holder_index[:, 0]
    request_index = jnp.arange(REQ_DEV, dtype=jnp.int32)
    earlier = (owners[None, :] == owners[:, None]) & (
        request_index[None, :] < request_index[:, None]
    )
    rank_among = jnp.sum(earlier.astype(jnp.int32), axis=1)
    matches = (owners[None, None, :] == jnp.arange(peers, dtype=jnp.int32)[:, None, None]) & (
        rank_among[None, None, :] == jnp.arange(request_cap, dtype=jnp.int32)[None, :, None]
    )
    present = jnp.any(matches, axis=2)
    chosen = jnp.sum(matches.astype(jnp.int32) * request_index[None, None, :], axis=2)
    offsets = jnp.arange(LMAX, dtype=jnp.int32)
    live = present[:, :, None] & (offsets[None, None, :] < lengths_row[chosen][:, :, None])
    source_row = jnp.where(
        live, prompt_starts[chosen][:, :, None] + offsets[None, None, :], 0
    ).reshape(peers, slots)
    slot_ids = jnp.where(live, adapter_place_index[chosen][:, :, None], -1).reshape(peers, slots, 1)
    send_rows = jnp.where(
        live.reshape(peers, slots)[:, :, None], tokens[source_row], jnp.zeros((), jnp.bfloat16)
    )
    base_output = jnp.dot(
        lax.all_gather(tokens, "mp", axis=1, tiled=True),
        value_weight,
        preferred_element_type=jnp.float32,
    )
    down_factor_sets = jnp.transpose(adapter_down_weight, (1, 0, 2))

    def mp_total(partial_value):
        return lax.psum(partial_value, "mp")

    adapter_update = grouped_update(
        lax.all_to_all(send_rows, "req", split_axis=0, concat_axis=0, tiled=True),
        lax.all_to_all(slot_ids, "req", split_axis=0, concat_axis=0, tiled=True),
        down_factor_sets,
        adapter_up_weight,
        mp_total,
    )
    value_output = lax.all_to_all(adapter_update, "req", split_axis=0, concat_axis=0, tiled=True)
    position = jnp.arange(tok_rows, dtype=jnp.int32)
    request_of = jnp.sum((position[:, None] >= prompt_ends[None, :]).astype(jnp.int32), axis=1)
    flat_index = (
        owners[request_of] * slots
        + rank_among[request_of] * LMAX
        + position
        - prompt_starts[request_of]
    )
    gathered_terms = value_output.reshape(peers * slots, value_output.shape[2])[flat_index]
    return (base_output + 0.5 * gathered_terms.astype(jnp.float32)).astype(jnp.bfloat16)


def gather_body(mesh, *args):
    tokens, lengths, holder, place, value_weight, down, up = args
    peers, mp = mesh.shape["req"], mesh.shape["mp"]
    rows, feats = tokens.shape
    held, rank, cols = up.shape
    down_rows = jnp.transpose(down, (1, 2, 0)).reshape(held * rank, feats)
    up_rows = up.reshape(held * rank, cols)
    anywhere = pl.BlockSpec(memory_space=pl.ANY)
    vmem = pl.BlockSpec(memory_space=pltpu.VMEM)
    dma = pltpu.SemaphoreType.DMA
    hops = max(peers - 1, 1)
    return pl.pallas_call(
        functools.partial(adapter_kernel, peers, held, rank),
        out_shape=jax.ShapeDtypeStruct((rows, cols), jnp.bfloat16),
        in_specs=[anywhere, vmem, vmem, vmem, anywhere, anywhere, anywhere],
        out_specs=vmem,
        scratch_shapes=[
            pltpu.VMEM((mp, rows, feats), jnp.bfloat16),
            pltpu.VMEM(value_weight.shape, jnp.bfloat16),
            pltpu.VMEM((peers, held * rank, feats), jnp.bfloat16),
            pltpu.VMEM((peers, held * rank, cols), jnp.bfloat16),
            pltpu.VMEM((mp, rows // 2, 2 * rank), jnp.bfloat16),
            pltpu.VMEM((rows, cols), jnp.float32),
            pltpu.VMEM((rows // 2, 2 * rank), jnp.float32),
            pltpu.VMEM((rows, 1), jnp.int32),
            dma((4,)),
            dma((2, hops, PIECES + 1)),
            dma((2, hops, PIECES + 1)),
            dma((2, hops, PIECES + 1)),
            dma((2, hops, PIECES + 1)),
            dma((3, SLICES)),
            dma((3, SLICES)),
            dma((3,)),
            dma((3,)),
        ],
        compiler_params=pltpu.CompilerParams(
            collective_id=0, has_side_effects=True, vmem_limit_bytes=48 << 20
        ),
        cost_estimate=pl.CostEstimate(
            flops=2 * rows * feats * (mp * cols + peers * held * rank),
            bytes_accessed=2 * (rows * feats + value_weight.size + down.size + up.size),
            transcendentals=0,
        ),
    )(
        tokens,
        lengths,
        holder.reshape(1, -1),
        place.reshape(1, -1),
        value_weight,
        down_rows,
        up_rows,
    )


def solution(mesh):
    placed = (
        P(("groups", "req"), "mp"),
        P(("groups", "req"), None),
        P(("groups", "req"), None),
        P(("groups", "req")),
        P(None, "mp"),
        P("mp", "req", None),
        P("req", None, "mp"),
    )

    def whole(*args):
        peers = mesh.shape["req"]
        moved = 2 * (args[5].size // mesh.shape["mp"] + args[6].size // mesh.shape["mp"])
        fits = moved <= GATHER_BYTES and peers > 1
        if fits and mesh.shape["mp"] == 4 and mesh.shape["groups"] == 2:
            part = functools.partial(gather_body, mesh)
        else:
            part = body
        return jax.shard_map(
            part, mesh=mesh, in_specs=placed, out_specs=P(("groups", "req"), "mp"), check_vma=False
        )(*args)

    return whole
```

```python
import functools

import jax
import jax.numpy as jnp
from jax import lax
from jax.experimental import pallas as pl
from jax.experimental.pallas import tpu as pltpu
from jax.sharding import PartitionSpec as P

LMAX = 4
REQ_DEV = 128
GATHER_BYTES = 24 << 20

PIECES = 4
SLICES = 4
MESH = pl.DeviceIdType.MESH


def adapter_kernel(
    peers,
    held,
    rank,
    tok,
    lengths,
    holder,
    place,
    weight,
    down,
    up,
    out,
    tok_all,
    tok_other,
    weight_here,
    down_all,
    up_all,
    low_all,
    low_sent,
    base,
    low_sum,
    small,
    prompts_of,
    adapter_of,
    local_sem,
    prompt_send_sem,
    prompt_recv_sem,
    t_send_sem,
    t_recv_sem,
    z_send_sem,
    z_recv_sem,
    y_send_sem,
    y_recv_sem,
    x_send_sem,
    x_recv_sem,
    low_send_sem,
    low_recv_sem,
):
    rows, feats = tok.shape
    cols = out.shape[1]
    part_rank = rank // 2
    packed = 2 * rank // part_rank
    width = held * part_rank
    quarter = rows // packed
    piece = feats // PIECES
    batch = rows // SLICES
    g, z, m = lax.axis_index("groups"), lax.axis_index("req"), lax.axis_index("mp")
    sibling = m + 1 - 2 * lax.rem(m, 2)
    across = lax.rem(m + 2, 4)
    diagonal = lax.rem(sibling + 2, 4)

    def remote(src, dst, send_sem, recv_sem, device):
        return pltpu.make_async_remote_copy(
            src_ref=src,
            dst_ref=dst,
            send_sem=send_sem,
            recv_sem=recv_sem,
            device_id=device,
            device_id_type=MESH,
        )

    def strip(h, side, c):
        if c < PIECES:
            return down_all.at[h, :, :, pl.ds(c * piece, piece)]
        lanes = pl.ds(pl.multiple_of(side * (cols // 2), 128), cols // 2)
        return up_all.at[h, :, lanes]

    def ranks_of(side):
        return pl.ds(pl.multiple_of(side * part_rank, 16), part_rank)

    def own_strip(c):
        if c < PIECES:
            return down.at[:, ranks_of(g), pl.ds(c * piece, piece)]
        lanes = pl.ds(pl.multiple_of(g * (cols // 2), 128), cols // 2)
        return up.at[:, lanes]

    def step_of(way):
        return 1 if way == 0 else -1

    def has(way, d):
        return z >= d if way == 0 else z + d <= peers - 1

    def upstream(way):
        return z if way == 0 else peers - 1 - z

    def has_next(way):
        return z + 1 <= peers - 1 if way == 0 else z >= 1

    def z_send(way, d, c):
        h = z - step_of(way) * d
        target = strip(h, g, c)
        return remote(
            own_strip(c) if d == 0 else target,
            target,
            z_send_sem.at[way, d, c],
            z_recv_sem.at[way, d, c],
            {"req": z + step_of(way)},
        )

    def z_recv(way, d, c):
        target = strip(z - step_of(way) * d, g, c)
        return remote(
            target,
            target,
            z_send_sem.at[way, d - 1, c],
            z_recv_sem.at[way, d - 1, c],
            {"req": z - step_of(way)},
        )

    def y_copy(way, d, side):
        target = strip(z - step_of(way) * d, side, PIECES)
        return remote(
            target,
            target,
            y_send_sem.at[way, d - 1],
            y_recv_sem.at[way, d - 1],
            {"groups": 1 - g},
        )

    def t_copy(s):
        there = pl.ds(s * batch, batch)
        return remote(
            tok.at[there],
            tok_other.at[there],
            t_send_sem.at[s],
            t_recv_sem.at[s],
            {"groups": 1 - g},
        )

    def pass_on(way, d, c, when):
        @pl.when(when)
        def _():
            z_recv(way, d, c).wait_recv()
            if d < peers - 1:
                pl.when(has_next(way))(z_send(way, d, c).start)
            if c == PIECES:
                y_copy(way, d, g).start()

    def batch_of(b, s):
        return tok_all.at[b, pl.ds(s * batch, batch)]

    def x_copy(kind, s):
        if kind == 2:
            src = batch_of(across, s)
        else:
            src = tok.at[pl.ds(s * batch, batch)]
        return remote(
            src,
            batch_of(across if kind == 2 else m, s),
            x_send_sem.at[kind, s],
            x_recv_sem.at[kind, s],
            {"mp": across if kind == 0 else sibling},
        )

    def x_recv(kind, s):
        target = batch_of((across, sibling, diagonal)[kind], s)
        return remote(
            target,
            target,
            x_send_sem.at[kind, s],
            x_recv_sem.at[kind, s],
            {"mp": across if kind == 0 else sibling},
        )

    others = (across, sibling, diagonal)
    low_device = [{"mp": b} for b in others] + [{"groups": 1 - g, "mp": b} for b in others + (m,)]

    def low_copy(i):
        return remote(
            low_sent.at[0 if i < 3 else 1],
            low_all.at[g, m],
            low_send_sem.at[i],
            low_recv_sem.at[i],
            low_device[i],
        )

    def low_recv(i):
        target = low_all.at[g if i < 3 else 1 - g, (others + others + (m,))[i]]
        return remote(target, target, low_send_sem.at[i], low_recv_sem.at[i], low_device[i])

    local = [
        pltpu.make_async_copy(lengths, small.at[0], local_sem.at[0]),
        pltpu.make_async_copy(holder, small.at[1], local_sem.at[1]),
        pltpu.make_async_copy(place, small.at[2], local_sem.at[2]),
        pltpu.make_async_copy(tok, tok_all.at[m], local_sem.at[3]),
        pltpu.make_async_copy(down.at[:, ranks_of(g)], down_all.at[z], local_sem.at[4]),
        pltpu.make_async_copy(weight, weight_here, local_sem.at[5]),
        pltpu.make_async_copy(up, up_all.at[z], local_sem.at[6]),
    ]
    for copy in local:
        copy.start()

    barrier = pltpu.get_barrier_semaphore()
    for device in low_device:
        pl.semaphore_signal(barrier, inc=1, device_id=device, device_id_type=MESH)
    for way in range(2):

        @pl.when(has_next(way))
        def _(way=way):
            pl.semaphore_signal(
                barrier, inc=1, device_id={"req": z + step_of(way)}, device_id_type=MESH
            )

    prompts = lengths.shape[1]
    for copy in local[:3]:
        copy.wait()
    lens = small[0]
    adapter = small[1] * held + small[2]
    row = lax.broadcasted_iota(jnp.int32, (8, prompts), 0)
    prompts_of[0] = jnp.where(row == 0, lens, adapter)

    beside = lax.div(z + peers - 1, peers) + lax.div(2 * peers - 2 - z, peers)
    pl.semaphore_wait(barrier, 7 + beside)

    for c in range(PIECES):
        for way in range(2):
            pl.when(has_next(way))(z_send(way, 0, c).start)
    for way in range(2):
        pl.when(has_next(way) & (upstream(way) == 0))(z_send(way, 0, PIECES).start)
    prompt_copy = remote(
        prompts_of.at[0],
        prompts_of.at[1],
        prompt_send_sem.at[0],
        prompt_recv_sem.at[0],
        {"groups": 1 - g},
    )
    prompt_copy.start()
    for s in range(SLICES):
        x_copy(0, s).start()
    for s in range(SLICES):
        t_copy(s).start()
    for s in range(SLICES):
        x_copy(1, s).start()

    def name_adapters(which):
        lens = prompts_of[which, 0:1]
        earlier = lax.broadcasted_iota(jnp.int32, (prompts, prompts), 0) <= lax.broadcasted_iota(
            jnp.int32, (prompts, prompts), 1
        )
        ends = jnp.dot(
            jnp.broadcast_to(lens, (8, prompts)).astype(jnp.float32).astype(jnp.bfloat16),
            earlier.astype(jnp.float32).astype(jnp.bfloat16),
            preferred_element_type=jnp.float32,
        )[0:1].astype(jnp.int32)
        position = lax.broadcasted_iota(jnp.int32, (rows, prompts), 0)
        inside = (position < ends) & (position >= ends - lens)
        named = jnp.where(inside, prompts_of[which, 1:2], 0)
        adapter_of[which] = jnp.sum(named, axis=1, keepdims=True)

    name_adapters(0)

    def add_base(b, first=False):
        term = jnp.dot(
            tok_all[b],
            weight_here[pl.ds(pl.multiple_of(b * feats, 128), feats)],
            preferred_element_type=jnp.float32,
        )
        if first:
            base[...] = term
        else:
            base[...] += term

    def member(which, h, part, per):
        lane = lax.broadcasted_iota(jnp.int32, (1, held * per), 1)
        owned = adapter_of[which, part * quarter : (part + 1) * quarter, :]
        return owned == lane // per + h * held

    def ones(shape, test):
        one, two = (lax.broadcasted_iota(jnp.int32, shape, axis) for axis in range(2))
        return test(one, two).astype(jnp.float32).astype(jnp.bfloat16)

    def add_low(which, h, first=False):
        partial = lax.dot_general(
            tok_all[m] if which == 0 else tok_other[...],
            down_all[h].reshape(width, feats),
            (((1,), (1,)), ((), ())),
            preferred_element_type=jnp.float32,
        )
        total = jnp.zeros((quarter, 2 * rank), jnp.float32)
        for part in range(packed):
            mine = partial[part * quarter : (part + 1) * quarter]
            kept = jnp.where(member(which, h, part, part_rank), mine, 0.0).astype(jnp.bfloat16)
            place_in = ones(
                (width, 2 * rank),
                lambda j, i: lax.rem(j, part_rank) == i - part * part_rank,
            )
            total += jnp.dot(kept, place_in, preferred_element_type=jnp.float32)
        if first:
            low_sum[which] = total
        else:
            low_sum[which] += total

    def add_held(which, way, d):
        @pl.when(has(way, d))
        def _():
            add_low(which, z - step_of(way) * d)

    local[3].wait()
    local[4].wait()
    add_low(0, z, first=True)
    local[5].wait()
    add_base(m, first=True)
    slot = 0
    for d in range(1, peers):
        for c in range(PIECES):
            for way in range(2):
                pass_on(way, d, c, has(way, d))
            if slot < SLICES:
                x_recv(0, slot).wait_recv()
                x_copy(2, slot).start()
            slot += 1
        for way in range(2):
            pl.when(has_next(way) & (upstream(way) == d))(z_send(way, 0, PIECES).start)
            for e in range(1, d):
                pass_on(way, e, PIECES, upstream(way) == d - 1)
        if d == 1:
            for s in range(SLICES):
                x_recv(1, s).wait_recv()
            add_base(sibling)
            add_base(across)
            prompt_copy.wait_recv()
            name_adapters(1)
        if d == 2:
            for s in range(SLICES):
                x_recv(2, s).wait_recv()
            add_base(diagonal)
        for way in range(2):
            add_held(0, way, d)
    for s in range(SLICES):
        t_copy(s).wait_recv()
    add_low(1, z, first=True)
    for d in range(1, peers):
        for way in range(2):
            add_held(1, way, d)

    low_sent[...] = low_sum[...].astype(jnp.bfloat16)
    for i in range(7):
        low_copy(i).start()
    low_all[g, m] = low_sent[0]
    for way in range(2):
        for e in range(1, peers):
            pass_on(way, e, PIECES, upstream(way) == peers - 1)
    for i in range(7):
        low_recv(i).wait_recv()
    lows = []
    for side in range(2):
        low = low_all[side, 0].astype(jnp.float32)
        for b in range(1, 4):
            low += low_all[side, b].astype(jnp.float32)
        lows.append(low.astype(jnp.bfloat16))
    low = jnp.concatenate(lows, axis=1)
    local[6].wait()
    for d in range(1, peers):
        for way in range(2):
            pl.when(has(way, d))(y_copy(way, d, 1 - g).wait_recv)
    for part in range(packed):

        def spread_at(i, j, part=part):
            inner = lax.rem(j, rank)
            side = inner // part_rank
            return i == side * (2 * rank) + part * part_rank + inner - side * part_rank

        spread = jnp.dot(
            low, ones((4 * rank, held * rank), spread_at), preferred_element_type=jnp.float32
        )
        term = jnp.zeros((quarter, cols), jnp.float32)
        for h in range(peers):
            kept = jnp.where(member(0, h, part, rank), spread, 0.0).astype(jnp.bfloat16)
            term += jnp.dot(kept, up_all[h], preferred_element_type=jnp.float32)
        term = term.astype(jnp.bfloat16).astype(jnp.float32)
        here = pl.ds(part * quarter, quarter)
        out[here, :] = (base[here, :] + 0.5 * term).astype(jnp.bfloat16)

    prompt_copy.wait_send()
    for s in range(SLICES):
        t_copy(s).wait_send()
    for s in range(SLICES):
        for kind in range(3):
            x_copy(kind, s).wait_send()
    for i in range(7):
        low_copy(i).wait_send()
    for way in range(2):
        for c in range(PIECES + 1):
            for d in range(peers - 1):
                sent = has_next(way) if d == 0 else has_next(way) & has(way, d)
                pl.when(sent)(z_send(way, d, c).wait_send)
        for d in range(1, peers):
            pl.when(has(way, d))(y_copy(way, d, g).wait_send)


def grouped_update(token_rows, slot_ids, down_factor_sets, up_sets, reduce_fn):
    count = token_rows.shape[0] * token_rows.shape[1]
    flat_rows = token_rows.reshape(count, token_rows.shape[2])
    flat_ids = slot_ids.reshape(count)
    held = down_factor_sets.shape[0]
    blocks = (count + 127) // 128 + held
    grouped = blocks * 128
    valid = flat_ids >= 0
    member = (flat_ids[:, None] == jnp.arange(held, dtype=jnp.int32)[None, :]).astype(jnp.int32)
    group_sizes = jnp.sum(member, axis=0)
    padded = (group_sizes + 127) // 128 * 128
    group_end = jnp.cumsum(padded)
    group_start = group_end - padded
    within = jnp.sum(jnp.cumsum(member, axis=0) * member, axis=1) - 1
    target = jnp.where(valid, jnp.sum(member * group_start[None, :], axis=1) + within, grouped)
    source = (
        jnp.zeros((grouped,), jnp.int32)
        .at[target]
        .set(jnp.arange(count, dtype=jnp.int32), mode="drop")
    )
    filled = jnp.zeros((grouped,), jnp.bool_).at[target].set(True, mode="drop")
    grouped_rows = jnp.where(filled[:, None], flat_rows[source], jnp.zeros((), jnp.bfloat16))
    grouped_rows = grouped_rows.reshape(blocks, 128, flat_rows.shape[1])
    block_first = jnp.arange(blocks, dtype=jnp.int32) * 128
    block_adapter = jnp.minimum(
        jnp.sum((block_first[:, None] >= group_end[None, :]).astype(jnp.int32), axis=1), held - 1
    )
    partial_value = jnp.einsum(
        "bkf,bfr->bkr",
        grouped_rows,
        down_factor_sets[block_adapter],
        preferred_element_type=jnp.float32,
    )
    reduced_rank_output = reduce_fn(partial_value).astype(jnp.bfloat16)
    term = jnp.einsum(
        "bkr,brc->bkc",
        reduced_rank_output,
        up_sets[block_adapter],
        preferred_element_type=jnp.float32,
    )
    term = term.astype(jnp.bfloat16).reshape(grouped, up_sets.shape[2])
    picked = jnp.where(
        valid[:, None], term[jnp.minimum(target, grouped - 1)], jnp.zeros((), jnp.bfloat16)
    )
    return picked.reshape(token_rows.shape[0], token_rows.shape[1], up_sets.shape[2])


def body(
    tokens,
    lengths,
    adapter_holder_index,
    adapter_place_index,
    value_weight,
    adapter_down_weight,
    adapter_up_weight,
):
    tok_rows = tokens.shape[0]
    peers = lax.axis_size("req")
    request_cap = max(2, REQ_DEV // peers + 1)
    slots = request_cap * LMAX
    lengths_row = lengths[0]
    prompt_ends = jnp.cumsum(lengths_row)
    prompt_starts = prompt_ends - lengths_row
    owners = adapter_holder_index[:, 0]
    request_index = jnp.arange(REQ_DEV, dtype=jnp.int32)
    earlier = (owners[None, :] == owners[:, None]) & (
        request_index[None, :] < request_index[:, None]
    )
    rank_among = jnp.sum(earlier.astype(jnp.int32), axis=1)
    matches = (owners[None, None, :] == jnp.arange(peers, dtype=jnp.int32)[:, None, None]) & (
        rank_among[None, None, :] == jnp.arange(request_cap, dtype=jnp.int32)[None, :, None]
    )
    present = jnp.any(matches, axis=2)
    chosen = jnp.sum(matches.astype(jnp.int32) * request_index[None, None, :], axis=2)
    offsets = jnp.arange(LMAX, dtype=jnp.int32)
    live = present[:, :, None] & (offsets[None, None, :] < lengths_row[chosen][:, :, None])
    source_row = jnp.where(
        live, prompt_starts[chosen][:, :, None] + offsets[None, None, :], 0
    ).reshape(peers, slots)
    slot_ids = jnp.where(live, adapter_place_index[chosen][:, :, None], -1).reshape(peers, slots, 1)
    send_rows = jnp.where(
        live.reshape(peers, slots)[:, :, None], tokens[source_row], jnp.zeros((), jnp.bfloat16)
    )
    base_output = jnp.dot(
        lax.all_gather(tokens, "mp", axis=1, tiled=True),
        value_weight,
        preferred_element_type=jnp.float32,
    )
    down_factor_sets = jnp.transpose(adapter_down_weight, (1, 0, 2))

    def mp_total(partial_value):
        return lax.psum(partial_value, "mp")

    adapter_update = grouped_update(
        lax.all_to_all(send_rows, "req", split_axis=0, concat_axis=0, tiled=True),
        lax.all_to_all(slot_ids, "req", split_axis=0, concat_axis=0, tiled=True),
        down_factor_sets,
        adapter_up_weight,
        mp_total,
    )
    value_output = lax.all_to_all(adapter_update, "req", split_axis=0, concat_axis=0, tiled=True)
    position = jnp.arange(tok_rows, dtype=jnp.int32)
    request_of = jnp.sum((position[:, None] >= prompt_ends[None, :]).astype(jnp.int32), axis=1)
    flat_index = (
        owners[request_of] * slots
        + rank_among[request_of] * LMAX
        + position
        - prompt_starts[request_of]
    )
    gathered_terms = value_output.reshape(peers * slots, value_output.shape[2])[flat_index]
    return (base_output + 0.5 * gathered_terms.astype(jnp.float32)).astype(jnp.bfloat16)


def gather_body(mesh, *args):
    tokens, lengths, holder, place, value_weight, down, up = args
    peers, mp = mesh.shape["req"], mesh.shape["mp"]
    rows, feats = tokens.shape
    held, rank, cols = up.shape
    prompts = lengths.shape[1]
    down_rows = jnp.transpose(down, (1, 2, 0))
    up_rows = up.reshape(held * rank, cols)
    anywhere = pl.BlockSpec(memory_space=pltpu.HBM)
    vmem = pl.BlockSpec(memory_space=pltpu.VMEM)
    dma = pltpu.SemaphoreType.DMA
    hops = max(peers - 1, 1)
    return pl.pallas_call(
        functools.partial(adapter_kernel, peers, held, rank),
        out_shape=jax.ShapeDtypeStruct((rows, cols), jnp.bfloat16),
        in_specs=[anywhere] * 7,
        out_specs=vmem,
        scratch_shapes=[
            pltpu.VMEM((mp, rows, feats), jnp.bfloat16),
            pltpu.VMEM((rows, feats), jnp.bfloat16),
            pltpu.VMEM(value_weight.shape, jnp.bfloat16),
            pltpu.VMEM((peers, held, rank // 2, feats), jnp.bfloat16),
            pltpu.VMEM((peers, held * rank, cols), jnp.bfloat16),
            pltpu.VMEM((2, mp, rows // 4, 2 * rank), jnp.bfloat16),
            pltpu.VMEM((2, rows // 4, 2 * rank), jnp.bfloat16),
            pltpu.VMEM((rows, cols), jnp.float32),
            pltpu.VMEM((2, rows // 4, 2 * rank), jnp.float32),
            pltpu.VMEM((3, 1, prompts), jnp.int32),
            pltpu.VMEM((2, 8, prompts), jnp.int32),
            pltpu.VMEM((2, rows, 1), jnp.int32),
            dma((7,)),
            dma((1,)),
            dma((1,)),
            dma((SLICES,)),
            dma((SLICES,)),
            dma((2, hops, PIECES + 1)),
            dma((2, hops, PIECES + 1)),
            dma((2, hops)),
            dma((2, hops)),
            dma((3, SLICES)),
            dma((3, SLICES)),
            dma((7,)),
            dma((7,)),
        ],
        compiler_params=pltpu.CompilerParams(
            collective_id=0, has_side_effects=True, vmem_limit_bytes=63 << 20
        ),
        cost_estimate=pl.CostEstimate(
            flops=2 * rows * feats * (mp * cols + peers * held * rank),
            bytes_accessed=2 * (rows * feats + value_weight.size + down.size + up.size),
            transcendentals=0,
        ),
    )(
        tokens,
        lengths,
        holder.reshape(1, -1),
        place.reshape(1, -1),
        value_weight,
        down_rows,
        up_rows,
    )


def solution(mesh):
    placed = (
        P(("groups", "req"), "mp"),
        P(("groups", "req"), None),
        P(("groups", "req"), None),
        P(("groups", "req")),
        P(None, "mp"),
        P("mp", "req", None),
        P("req", None, "mp"),
    )

    def whole(*args):
        peers = mesh.shape["req"]
        moved = 2 * (args[5].size // mesh.shape["mp"] + args[6].size // mesh.shape["mp"])
        fits = moved <= GATHER_BYTES and peers > 1
        if fits and mesh.shape["mp"] == 4 and mesh.shape["groups"] == 2:
            part = functools.partial(gather_body, mesh)
        else:
            part = body
        return jax.shard_map(
            part, mesh=mesh, in_specs=placed, out_specs=P(("groups", "req"), "mp"), check_vma=False
        )(*args)

    return whole
```

```python
import functools

import jax
import jax.numpy as jnp
from jax import lax
from jax.experimental import pallas as pl
from jax.experimental.pallas import tpu as pltpu
from jax.sharding import PartitionSpec as P

LMAX = 4
REQ_DEV = 128
GATHER_BYTES = 24 << 20

PIECES = 4
SLICES = 4
MESH = pl.DeviceIdType.MESH


def adapter_kernel(
    peers,
    held,
    rank,
    tok,
    lengths,
    holder,
    place,
    weight,
    down,
    up,
    out,
    tok_all,
    tok_other,
    weight_here,
    down_all,
    up_all,
    low_all,
    low_sent,
    low_full,
    low_back,
    tok_end,
    prompts_end,
    base,
    low_sum,
    small,
    prompts_of,
    adapter_of,
    local_sem,
    prompt_send_sem,
    prompt_recv_sem,
    t_send_sem,
    t_recv_sem,
    z_send_sem,
    z_recv_sem,
    y_send_sem,
    y_recv_sem,
    x_send_sem,
    x_recv_sem,
    low_send_sem,
    low_recv_sem,
    full_send_sem,
    full_recv_sem,
    end_send_sem,
    end_recv_sem,
    back_send_sem,
    back_recv_sem,
):
    rows, feats = tok.shape
    cols = out.shape[1]
    width = held * rank
    half = rows // 2
    share = half // 4
    mine = feats // 2
    helped = mine // 2
    piece = mine // PIECES
    batch = rows // SLICES
    g, z, m = lax.axis_index("groups"), lax.axis_index("req"), lax.axis_index("mp")
    sibling = m + 1 - 2 * lax.rem(m, 2)
    across = lax.rem(m + 2, 4)
    diagonal = lax.rem(sibling + 2, 4)

    def remote(src, dst, send_sem, recv_sem, device):
        return pltpu.make_async_remote_copy(
            src_ref=src,
            dst_ref=dst,
            send_sem=send_sem,
            recv_sem=recv_sem,
            device_id=device,
            device_id_type=MESH,
        )

    def strip(h, side, c):
        if c < PIECES:
            return down_all.at[h, :, pl.ds(c * piece, piece)]
        lanes = pl.ds(pl.multiple_of(side * (cols // 2), 128), cols // 2)
        return up_all.at[h, :, lanes]

    def features(side, start, count):
        return pl.ds(pl.multiple_of(side * mine + start, 128), count)

    def own_strip(c):
        if c < PIECES:
            return down.at[:, features(g, c * piece, piece)]
        lanes = pl.ds(pl.multiple_of(g * (cols // 2), 128), cols // 2)
        return up.at[:, lanes]

    def inner(at):
        return (at >= 1) & (at <= peers - 2)

    is_end = (z == 0) | (z == peers - 1)
    is_helper = (z == 1) | (z == peers - 2)
    inward = 1 - 2 * lax.div(z, peers - 1)
    outward = 2 * lax.div(z, 2) - 1

    def helped_piece(c):
        return c * piece < helped and c < PIECES

    def step_of(way):
        return 1 if way == 0 else -1

    def has(way, d, c=PIECES):
        held_here = z >= d if way == 0 else z + d <= peers - 1
        return held_here & inner(z) if helped_piece(c) else held_here

    def upstream(way):
        return z if way == 0 else peers - 1 - z

    def has_next(way, c=PIECES):
        there = z + 1 <= peers - 1 if way == 0 else z >= 1
        return there & inner(z + step_of(way)) if helped_piece(c) else there

    def z_send(way, d, c):
        h = z - step_of(way) * d
        target = strip(h, g, c)
        return remote(
            own_strip(c) if d == 0 else target,
            target,
            z_send_sem.at[way, d, c],
            z_recv_sem.at[way, d, c],
            {"req": z + step_of(way)},
        )

    def z_recv(way, d, c):
        target = strip(z - step_of(way) * d, g, c)
        return remote(
            target,
            target,
            z_send_sem.at[way, d - 1, c],
            z_recv_sem.at[way, d - 1, c],
            {"req": z - step_of(way)},
        )

    def y_copy(way, d, side):
        target = strip(z - step_of(way) * d, side, PIECES)
        return remote(
            target,
            target,
            y_send_sem.at[way, d - 1],
            y_recv_sem.at[way, d - 1],
            {"groups": 1 - g},
        )

    def t_copy(s):
        return remote(
            tok.at[:, features(1 - g, s * helped, helped)],
            tok_other.at[:, pl.ds(s * helped, helped)],
            t_send_sem.at[s],
            t_recv_sem.at[s],
            {"groups": 1 - g},
        )

    def end_copy(i):
        sources = (
            tok.at[:, features(g, 0, helped)],
            tok_other.at[:, pl.ds(0, helped)],
            prompts_of,
        )
        targets = (tok_end.at[0], tok_end.at[1], prompts_end)
        return remote(
            sources[i],
            targets[i],
            end_send_sem.at[i],
            end_recv_sem.at[i],
            {"req": z + inward},
        )

    def end_recv(i):
        target = (tok_end.at[0], tok_end.at[1], prompts_end)[i]
        return remote(
            target, target, end_send_sem.at[i], end_recv_sem.at[i], {"req": z + outward}
        )

    def back_copy(i):
        return remote(
            low_back.at[0, i],
            low_back.at[1, i],
            back_send_sem.at[i],
            back_recv_sem.at[i],
            {"req": z + outward},
        )

    def back_recv(i):
        target = low_back.at[1, i]
        return remote(
            target, target, back_send_sem.at[i], back_recv_sem.at[i], {"req": z + inward}
        )

    def pass_on(way, d, c, when):
        @pl.when(when)
        def _():
            z_recv(way, d, c).wait_recv()
            if d < peers - 1:
                pl.when(has_next(way, c))(z_send(way, d, c).start)
            if c == PIECES:
                y_copy(way, d, g).start()

    def batch_of(b, s):
        return tok_all.at[b, pl.ds(s * batch, batch)]

    def x_copy(kind, s):
        if kind == 2:
            src = batch_of(across, s)
        else:
            src = tok.at[pl.ds(s * batch, batch)]
        return remote(
            src,
            batch_of(across if kind == 2 else m, s),
            x_send_sem.at[kind, s],
            x_recv_sem.at[kind, s],
            {"mp": across if kind == 0 else sibling},
        )

    def x_recv(kind, s):
        target = batch_of((across, sibling, diagonal)[kind], s)
        return remote(
            target,
            target,
            x_send_sem.at[kind, s],
            x_recv_sem.at[kind, s],
            {"mp": across if kind == 0 else sibling},
        )

    others = (across, sibling, diagonal)
    low_device = [{"mp": b} for b in others] + [{"groups": 1 - g, "mp": b} for b in others + (m,)]

    def share_of(b):
        return pl.ds(pl.multiple_of(b * share, 16), share)

    def low_copy(i):
        return remote(
            low_sent.at[0 if i < 3 else 1, share_of((others + others + (m,))[i])],
            low_all.at[g, m],
            low_send_sem.at[i],
            low_recv_sem.at[i],
            low_device[i],
        )

    def low_recv(i):
        target = low_all.at[g if i < 3 else 1 - g, (others + others + (m,))[i]]
        return remote(target, target, low_send_sem.at[i], low_recv_sem.at[i], low_device[i])

    def full_copy(i):
        here = low_full.at[share_of(m)]
        return remote(here, here, full_send_sem.at[i], full_recv_sem.at[i], low_device[i])

    def full_recv(i):
        target = low_full.at[share_of(others[i])]
        return remote(target, target, full_send_sem.at[i], full_recv_sem.at[i], low_device[i])

    local = [
        pltpu.make_async_copy(lengths, small.at[0], local_sem.at[0]),
        pltpu.make_async_copy(holder, small.at[1], local_sem.at[1]),
        pltpu.make_async_copy(place, small.at[2], local_sem.at[2]),
        pltpu.make_async_copy(tok, tok_all.at[m], local_sem.at[3]),
        pltpu.make_async_copy(down.at[:, features(g, 0, mine)], down_all.at[z], local_sem.at[4]),
        pltpu.make_async_copy(weight, weight_here, local_sem.at[5]),
        pltpu.make_async_copy(up, up_all.at[z], local_sem.at[6]),
    ]
    for copy in local:
        copy.start()

    barrier = pltpu.get_barrier_semaphore()
    for device in low_device:
        pl.semaphore_signal(barrier, inc=1, device_id=device, device_id_type=MESH)
    for way in range(2):

        @pl.when(has_next(way))
        def _(way=way):
            pl.semaphore_signal(
                barrier, inc=1, device_id={"req": z + step_of(way)}, device_id_type=MESH
            )

    prompts = lengths.shape[1]
    for copy in local[:3]:
        copy.wait()
    lens = small[0]
    adapter = small[1] * held + small[2]
    row = lax.broadcasted_iota(jnp.int32, (8, prompts), 0)
    prompts_of[0] = jnp.where(row == 0, lens, adapter)

    beside = lax.div(z + peers - 1, peers) + lax.div(2 * peers - 2 - z, peers)
    pl.semaphore_wait(barrier, 7 + beside)

    pl.when(is_end)(end_copy(0).start)
    for c in range(PIECES):
        for way in range(2):
            pl.when(has_next(way, c))(z_send(way, 0, c).start)
    for way in range(2):
        pl.when(has_next(way) & (upstream(way) == 0))(z_send(way, 0, PIECES).start)
    prompt_copy = remote(
        prompts_of.at[0],
        prompts_of.at[1],
        prompt_send_sem.at[0],
        prompt_recv_sem.at[0],
        {"groups": 1 - g},
    )
    prompt_copy.start()
    for s in range(SLICES):
        x_copy(0, s).start()
    for s in range(2):
        t_copy(s).start()
    for s in range(SLICES):
        x_copy(1, s).start()

    def name_adapters(which):
        table = prompts_of if which < 2 else prompts_end
        lens = table[which % 2, 0:1]
        earlier = lax.broadcasted_iota(jnp.int32, (prompts, prompts), 0) <= lax.broadcasted_iota(
            jnp.int32, (prompts, prompts), 1
        )
        ends = jnp.dot(
            jnp.broadcast_to(lens, (8, prompts)).astype(jnp.float32).astype(jnp.bfloat16),
            earlier.astype(jnp.float32).astype(jnp.bfloat16),
            preferred_element_type=jnp.float32,
        )[0:1].astype(jnp.int32)
        position = lax.broadcasted_iota(jnp.int32, (rows, prompts), 0)
        inside = (position < ends) & (position >= ends - lens)
        named = jnp.where(inside, table[which % 2, 1:2], 0)
        adapter_of[which] = jnp.sum(named, axis=1, keepdims=True)

    name_adapters(0)

    def add_base(b, first=False):
        term = jnp.dot(
            tok_all[b],
            weight_here[pl.ds(pl.multiple_of(b * feats, 128), feats)],
            preferred_element_type=jnp.float32,
        )
        if first:
            base[...] = term
        else:
            base[...] += term

    def member(which, h, part):
        lane = lax.broadcasted_iota(jnp.int32, (1, width), 1)
        return adapter_of[which, part * half : (part + 1) * half, :] == lane // rank + h * held

    def fold(part, turned):
        shape = (2 * rank, width) if turned else (width, 2 * rank)
        one = lax.broadcasted_iota(jnp.int32, shape, 1 if turned else 0)
        two = lax.broadcasted_iota(jnp.int32, shape, 0 if turned else 1)
        return (lax.rem(one, rank) == two - part * rank).astype(jnp.float32).astype(jnp.bfloat16)

    def add_low(which, h, start, count, first=False):
        if which == 0:
            features_here = tok_all[m, :, features(g, start, count)]
        elif which == 1:
            features_here = tok_other[:, start : start + count]
        else:
            features_here = tok_end[which - 2]
        partial = lax.dot_general(
            features_here,
            down_all[h, :, start : start + count],
            (((1,), (1,)), ((), ())),
            preferred_element_type=jnp.float32,
        )
        total = jnp.zeros((half, 2 * rank), jnp.float32)
        for part in range(2):
            ours = partial[part * half : (part + 1) * half]
            kept = jnp.where(member(which, h, part), ours, 0.0).astype(jnp.bfloat16)
            total += jnp.dot(kept, fold(part, False), preferred_element_type=jnp.float32)
        if first:
            low_sum[which] = total
        else:
            low_sum[which] += total

    def add_held(which, way, d):
        h = z - step_of(way) * d
        pl.when(has(way, d) & inner(z))(lambda: add_low(which, h, 0, mine))
        pl.when(has(way, d) & is_end)(lambda: add_low(which, h, helped, helped))

    def help_end(i):
        @pl.when(is_helper)
        def _():
            end_recv(i).wait_recv()
            if i == 0:
                end_recv(2).wait_recv()
            name_adapters(2 + i)
            add_low(2 + i, z, 0, helped, first=True)
            for d in range(1, peers - 1):
                add_low(2 + i, z - outward * d, 0, helped)
            low_back[0, i] = low_sum[2 + i].astype(jnp.bfloat16)
            back_copy(i).start()

    local[3].wait()
    local[4].wait()
    add_low(0, z, 0, mine, first=True)
    local[5].wait()
    add_base(m, first=True)
    x_slots = {2: 0, 5: 1, 8: 2, 11: 3}
    slot = 0
    for d in range(1, peers):
        for way in range(2):
            for e in range(1, d):
                pass_on(way, e, PIECES, upstream(way) == d - 1)
        if d == peers - 1:
            help_end(0)
            help_end(1)
        for c in range(PIECES):
            for way in range(2):
                pass_on(way, d, c, has(way, d, c))
            if slot in x_slots:
                x_recv(0, x_slots[slot]).wait_recv()
                x_copy(2, x_slots[slot]).start()
            if slot == 1:
                prompt_copy.wait_recv()
                t_copy(0).wait_recv()

                @pl.when(is_end)
                def _():
                    end_copy(2).start()
                    end_copy(1).start()

            slot += 1
        for way in range(2):
            pl.when(has_next(way) & (upstream(way) == d))(z_send(way, 0, PIECES).start)
        if d == 1:
            name_adapters(1)
            t_copy(1).wait_recv()
            add_low(1, z, 0, mine, first=True)
            for s in range(SLICES):
                x_recv(1, s).wait_recv()
            add_base(sibling)
        for way in range(2):
            for which in range(2):
                add_held(which, way, d)

    @pl.when(is_end)
    def _():
        for i in range(2):
            back_recv(i).wait_recv()
            low_sum[i] += low_back[1, i].astype(jnp.float32)

    low_sent[...] = low_sum[0:2].astype(jnp.bfloat16)
    for i in range(7):
        low_copy(i).start()
    low_all[g, m] = low_sent[0, share_of(m)]
    add_base(across)
    for way in range(2):
        for e in range(1, peers):
            pass_on(way, e, PIECES, upstream(way) == peers - 1)
    for i in range(7):
        low_recv(i).wait_recv()
    low = low_all[0, 0].astype(jnp.float32)
    for i in range(1, 8):
        low += low_all[i // 4, i % 4].astype(jnp.float32)
    low_full[share_of(m)] = low.astype(jnp.bfloat16)
    for i in range(3):
        full_copy(i).start()
    for s in range(SLICES):
        x_recv(2, s).wait_recv()
    add_base(diagonal)
    local[6].wait()
    for d in range(1, peers):
        for way in range(2):
            pl.when(has(way, d))(y_copy(way, d, 1 - g).wait_recv)
    for i in range(3):
        full_recv(i).wait_recv()
    low = low_full[...]
    for part in range(2):
        spread = jnp.dot(low, fold(part, True), preferred_element_type=jnp.float32)
        term = jnp.zeros((half, cols), jnp.float32)
        for h in range(peers):
            kept = jnp.where(member(0, h, part), spread, 0.0).astype(jnp.bfloat16)
            term += jnp.dot(kept, up_all[h], preferred_element_type=jnp.float32)
        term = term.astype(jnp.bfloat16).astype(jnp.float32)
        here = pl.ds(part * half, half)
        out[here, :] = (base[here, :] + 0.5 * term).astype(jnp.bfloat16)

    for i in range(3):
        full_copy(i).wait_send()
        pl.when(is_end)(end_copy(i).wait_send)
    for i in range(2):
        pl.when(is_helper)(back_copy(i).wait_send)
    prompt_copy.wait_send()
    for s in range(2):
        t_copy(s).wait_send()
    for s in range(SLICES):
        for kind in range(3):
            x_copy(kind, s).wait_send()
    for i in range(7):
        low_copy(i).wait_send()
    for way in range(2):
        for c in range(PIECES + 1):
            for d in range(peers - 1):
                sent = has_next(way, c) if d == 0 else has_next(way, c) & has(way, d, c)
                pl.when(sent)(z_send(way, d, c).wait_send)
        for d in range(1, peers):
            pl.when(has(way, d))(y_copy(way, d, g).wait_send)


def grouped_update(token_rows, slot_ids, down_factor_sets, up_sets, reduce_fn):
    count = token_rows.shape[0] * token_rows.shape[1]
    flat_rows = token_rows.reshape(count, token_rows.shape[2])
    flat_ids = slot_ids.reshape(count)
    held = down_factor_sets.shape[0]
    blocks = (count + 127) // 128 + held
    grouped = blocks * 128
    valid = flat_ids >= 0
    member = (flat_ids[:, None] == jnp.arange(held, dtype=jnp.int32)[None, :]).astype(jnp.int32)
    group_sizes = jnp.sum(member, axis=0)
    padded = (group_sizes + 127) // 128 * 128
    group_end = jnp.cumsum(padded)
    group_start = group_end - padded
    within = jnp.sum(jnp.cumsum(member, axis=0) * member, axis=1) - 1
    target = jnp.where(valid, jnp.sum(member * group_start[None, :], axis=1) + within, grouped)
    source = (
        jnp.zeros((grouped,), jnp.int32)
        .at[target]
        .set(jnp.arange(count, dtype=jnp.int32), mode="drop")
    )
    filled = jnp.zeros((grouped,), jnp.bool_).at[target].set(True, mode="drop")
    grouped_rows = jnp.where(filled[:, None], flat_rows[source], jnp.zeros((), jnp.bfloat16))
    grouped_rows = grouped_rows.reshape(blocks, 128, flat_rows.shape[1])
    block_first = jnp.arange(blocks, dtype=jnp.int32) * 128
    block_adapter = jnp.minimum(
        jnp.sum((block_first[:, None] >= group_end[None, :]).astype(jnp.int32), axis=1), held - 1
    )
    partial_value = jnp.einsum(
        "bkf,bfr->bkr",
        grouped_rows,
        down_factor_sets[block_adapter],
        preferred_element_type=jnp.float32,
    )
    reduced_rank_output = reduce_fn(partial_value).astype(jnp.bfloat16)
    term = jnp.einsum(
        "bkr,brc->bkc",
        reduced_rank_output,
        up_sets[block_adapter],
        preferred_element_type=jnp.float32,
    )
    term = term.astype(jnp.bfloat16).reshape(grouped, up_sets.shape[2])
    picked = jnp.where(
        valid[:, None], term[jnp.minimum(target, grouped - 1)], jnp.zeros((), jnp.bfloat16)
    )
    return picked.reshape(token_rows.shape[0], token_rows.shape[1], up_sets.shape[2])


def body(
    tokens,
    lengths,
    adapter_holder_index,
    adapter_place_index,
    value_weight,
    adapter_down_weight,
    adapter_up_weight,
):
    tok_rows = tokens.shape[0]
    peers = lax.axis_size("req")
    request_cap = max(2, REQ_DEV // peers + 1)
    slots = request_cap * LMAX
    lengths_row = lengths[0]
    prompt_ends = jnp.cumsum(lengths_row)
    prompt_starts = prompt_ends - lengths_row
    owners = adapter_holder_index[:, 0]
    request_index = jnp.arange(REQ_DEV, dtype=jnp.int32)
    earlier = (owners[None, :] == owners[:, None]) & (
        request_index[None, :] < request_index[:, None]
    )
    rank_among = jnp.sum(earlier.astype(jnp.int32), axis=1)
    matches = (owners[None, None, :] == jnp.arange(peers, dtype=jnp.int32)[:, None, None]) & (
        rank_among[None, None, :] == jnp.arange(request_cap, dtype=jnp.int32)[None, :, None]
    )
    present = jnp.any(matches, axis=2)
    chosen = jnp.sum(matches.astype(jnp.int32) * request_index[None, None, :], axis=2)
    offsets = jnp.arange(LMAX, dtype=jnp.int32)
    live = present[:, :, None] & (offsets[None, None, :] < lengths_row[chosen][:, :, None])
    source_row = jnp.where(
        live, prompt_starts[chosen][:, :, None] + offsets[None, None, :], 0
    ).reshape(peers, slots)
    slot_ids = jnp.where(live, adapter_place_index[chosen][:, :, None], -1).reshape(peers, slots, 1)
    send_rows = jnp.where(
        live.reshape(peers, slots)[:, :, None], tokens[source_row], jnp.zeros((), jnp.bfloat16)
    )
    base_output = jnp.dot(
        lax.all_gather(tokens, "mp", axis=1, tiled=True),
        value_weight,
        preferred_element_type=jnp.float32,
    )
    down_factor_sets = jnp.transpose(adapter_down_weight, (1, 0, 2))

    def mp_total(partial_value):
        return lax.psum(partial_value, "mp")

    adapter_update = grouped_update(
        lax.all_to_all(send_rows, "req", split_axis=0, concat_axis=0, tiled=True),
        lax.all_to_all(slot_ids, "req", split_axis=0, concat_axis=0, tiled=True),
        down_factor_sets,
        adapter_up_weight,
        mp_total,
    )
    value_output = lax.all_to_all(adapter_update, "req", split_axis=0, concat_axis=0, tiled=True)
    position = jnp.arange(tok_rows, dtype=jnp.int32)
    request_of = jnp.sum((position[:, None] >= prompt_ends[None, :]).astype(jnp.int32), axis=1)
    flat_index = (
        owners[request_of] * slots
        + rank_among[request_of] * LMAX
        + position
        - prompt_starts[request_of]
    )
    gathered_terms = value_output.reshape(peers * slots, value_output.shape[2])[flat_index]
    return (base_output + 0.5 * gathered_terms.astype(jnp.float32)).astype(jnp.bfloat16)


def gather_body(mesh, *args):
    tokens, lengths, holder, place, value_weight, down, up = args
    peers, mp = mesh.shape["req"], mesh.shape["mp"]
    rows, feats = tokens.shape
    held, rank, cols = up.shape
    prompts = lengths.shape[1]
    down_rows = jnp.transpose(down, (1, 2, 0)).reshape(held * rank, feats)
    up_rows = up.reshape(held * rank, cols)
    anywhere = pl.BlockSpec(memory_space=pltpu.HBM)
    vmem = pl.BlockSpec(memory_space=pltpu.VMEM)
    dma = pltpu.SemaphoreType.DMA
    hops = max(peers - 1, 1)
    return pl.pallas_call(
        functools.partial(adapter_kernel, peers, held, rank),
        out_shape=jax.ShapeDtypeStruct((rows, cols), jnp.bfloat16),
        in_specs=[anywhere] * 7,
        out_specs=vmem,
        scratch_shapes=[
            pltpu.VMEM((mp, rows, feats), jnp.bfloat16),
            pltpu.VMEM((rows, feats // 2), jnp.bfloat16),
            pltpu.VMEM(value_weight.shape, jnp.bfloat16),
            pltpu.VMEM((peers, held * rank, feats // 2), jnp.bfloat16),
            pltpu.VMEM((peers, held * rank, cols), jnp.bfloat16),
            pltpu.VMEM((2, mp, rows // 8, 2 * rank), jnp.bfloat16),
            pltpu.VMEM((2, rows // 2, 2 * rank), jnp.bfloat16),
            pltpu.VMEM((rows // 2, 2 * rank), jnp.bfloat16),
            pltpu.VMEM((2, 2, rows // 2, 2 * rank), jnp.bfloat16),
            pltpu.VMEM((2, rows, feats // 4), jnp.bfloat16),
            pltpu.VMEM((2, 8, prompts), jnp.int32),
            pltpu.VMEM((rows, cols), jnp.float32),
            pltpu.VMEM((4, rows // 2, 2 * rank), jnp.float32),
            pltpu.VMEM((3, 1, prompts), jnp.int32),
            pltpu.VMEM((2, 8, prompts), jnp.int32),
            pltpu.VMEM((4, rows, 1), jnp.int32),
            dma((7,)),
            dma((1,)),
            dma((1,)),
            dma((2,)),
            dma((2,)),
            dma((2, hops, PIECES + 1)),
            dma((2, hops, PIECES + 1)),
            dma((2, hops)),
            dma((2, hops)),
            dma((3, SLICES)),
            dma((3, SLICES)),
            dma((7,)),
            dma((7,)),
            dma((3,)),
            dma((3,)),
            dma((3,)),
            dma((3,)),
            dma((2,)),
            dma((2,)),
        ],
        compiler_params=pltpu.CompilerParams(
            collective_id=0, has_side_effects=True, vmem_limit_bytes=63 << 20
        ),
        cost_estimate=pl.CostEstimate(
            flops=2 * rows * feats * (mp * cols + peers * held * rank),
            bytes_accessed=2 * (rows * feats + value_weight.size + down.size + up.size),
            transcendentals=0,
        ),
    )(
        tokens,
        lengths,
        holder.reshape(1, -1),
        place.reshape(1, -1),
        value_weight,
        down_rows,
        up_rows,
    )


def solution(mesh):
    placed = (
        P(("groups", "req"), "mp"),
        P(("groups", "req"), None),
        P(("groups", "req"), None),
        P(("groups", "req")),
        P(None, "mp"),
        P("mp", "req", None),
        P("req", None, "mp"),
    )

    def whole(*args):
        peers = mesh.shape["req"]
        moved = 2 * (args[5].size // mesh.shape["mp"] + args[6].size // mesh.shape["mp"])
        fits = moved <= GATHER_BYTES and peers == 4
        if fits and mesh.shape["mp"] == 4 and mesh.shape["groups"] == 2:
            part = functools.partial(gather_body, mesh)
        else:
            part = body
        return jax.shard_map(
            part, mesh=mesh, in_specs=placed, out_specs=P(("groups", "req"), "mp"), check_vma=False
        )(*args)

    return whole
```

```python
import functools

import jax
import jax.numpy as jnp
from jax import lax
from jax.experimental import pallas as pl
from jax.experimental.pallas import tpu as pltpu
from jax.sharding import PartitionSpec as P

LMAX = 4
REQ_DEV = 128
GATHER_BYTES = 24 << 20

PIECES = 4
SLICES = 4
MESH = pl.DeviceIdType.MESH


def adapter_kernel(
    peers,
    held,
    rank,
    tok,
    lengths,
    holder,
    place,
    weight,
    down,
    up,
    out,
    tok_all,
    tok_other,
    weight_here,
    down_all,
    up_all,
    low_all,
    low_sent,
    low_full,
    low_back,
    tok_end,
    prompts_end,
    base,
    low_sum,
    small,
    prompts_of,
    adapter_of,
    local_sem,
    prompt_send_sem,
    prompt_recv_sem,
    t_send_sem,
    t_recv_sem,
    z_send_sem,
    z_recv_sem,
    y_send_sem,
    y_recv_sem,
    x_send_sem,
    x_recv_sem,
    low_send_sem,
    low_recv_sem,
    full_send_sem,
    full_recv_sem,
    end_send_sem,
    end_recv_sem,
    back_send_sem,
    back_recv_sem,
):
    rows, feats = tok.shape
    cols = out.shape[1]
    width = held * rank
    half = rows // 2
    share = half // 4
    mine = feats // 2
    helped = mine // 2
    batches = PIECES // 2
    piece = width // batches
    batch = rows // SLICES
    g, z, m = lax.axis_index("groups"), lax.axis_index("req"), lax.axis_index("mp")
    sibling = m + 1 - 2 * lax.rem(m, 2)
    across = lax.rem(m + 2, 4)
    diagonal = lax.rem(sibling + 2, 4)

    def remote(src, dst, send_sem, recv_sem, device):
        return pltpu.make_async_remote_copy(
            src_ref=src,
            dst_ref=dst,
            send_sem=send_sem,
            recv_sem=recv_sem,
            device_id=device,
            device_id_type=MESH,
        )

    def strip(h, side, c):
        if c < PIECES:
            return down_all.at[h, c // batches, pl.ds((c % batches) * piece, piece)]
        return up_all.at[h, up_rows(side)]

    def up_rows(side):
        return pl.ds(pl.multiple_of(side * (width // 2), 16), width // 2)

    def features(side, start, count):
        return pl.ds(pl.multiple_of(side * mine + start, 128), count)

    def own_strip(c):
        if c < PIECES:
            lanes = features(g, (c // batches) * helped, helped)
            return down.at[pl.ds((c % batches) * piece, piece), lanes]
        return up.at[up_rows(g)]

    def inner(at):
        return (at >= 1) & (at <= peers - 2)

    is_end = (z == 0) | (z == peers - 1)
    is_helper = (z == 1) | (z == peers - 2)
    inward = 1 - 2 * lax.div(z, peers - 1)
    outward = 2 * lax.div(z, 2) - 1

    def helped_piece(c):
        return batches <= c < PIECES

    def step_of(way):
        return 1 if way == 0 else -1

    def has(way, d, c=PIECES):
        held_here = z >= d if way == 0 else z + d <= peers - 1
        return held_here & inner(z) if helped_piece(c) else held_here

    def has_next(way, c=PIECES):
        there = z + 1 <= peers - 1 if way == 0 else z >= 1
        return there & inner(z + step_of(way)) if helped_piece(c) else there

    def z_send(way, d, c):
        h = z - step_of(way) * d
        target = strip(h, g, c)
        return remote(
            own_strip(c) if d == 0 else target,
            target,
            z_send_sem.at[way, d, c],
            z_recv_sem.at[way, d, c],
            {"req": z + step_of(way)},
        )

    def z_recv(way, d, c):
        target = strip(z - step_of(way) * d, g, c)
        return remote(
            target,
            target,
            z_send_sem.at[way, d - 1, c],
            z_recv_sem.at[way, d - 1, c],
            {"req": z - step_of(way)},
        )

    def y_copy(way, d, side):
        target = strip(z - step_of(way) * d, side, PIECES)
        return remote(
            target,
            target,
            y_send_sem.at[way, d - 1],
            y_recv_sem.at[way, d - 1],
            {"groups": 1 - g},
        )

    def t_copy(s):
        return remote(
            tok.at[:, features(1 - g, s * helped, helped)],
            tok_other.at[s],
            t_send_sem.at[s],
            t_recv_sem.at[s],
            {"groups": 1 - g},
        )

    def end_copy(i):
        sources = (
            tok.at[:, features(g, helped, helped)],
            tok_other.at[1],
            prompts_of,
        )
        targets = (tok_end.at[0], tok_end.at[1], prompts_end)
        return remote(
            sources[i],
            targets[i],
            end_send_sem.at[i],
            end_recv_sem.at[i],
            {"req": z + inward},
        )

    def end_recv(i):
        target = (tok_end.at[0], tok_end.at[1], prompts_end)[i]
        return remote(
            target, target, end_send_sem.at[i], end_recv_sem.at[i], {"req": z + outward}
        )

    def back_copy(i):
        return remote(
            low_back.at[0, i],
            low_back.at[1, i],
            back_send_sem.at[i],
            back_recv_sem.at[i],
            {"req": z + outward},
        )

    def back_recv(i):
        target = low_back.at[1, i]
        return remote(
            target, target, back_send_sem.at[i], back_recv_sem.at[i], {"req": z + inward}
        )

    def pass_on(way, d, c, when):
        @pl.when(when)
        def _():
            z_recv(way, d, c).wait_recv()
            if d < peers - 1:
                pl.when(has_next(way, c))(z_send(way, d, c).start)
            if c == PIECES:
                y_copy(way, d, g).start()

    def batch_of(b, s):
        return tok_all.at[b, pl.ds(s * batch, batch)]

    def x_copy(kind, s):
        if kind == 2:
            src = batch_of(across, s)
        else:
            src = tok.at[pl.ds(s * batch, batch)]
        return remote(
            src,
            batch_of(across if kind == 2 else m, s),
            x_send_sem.at[kind, s],
            x_recv_sem.at[kind, s],
            {"mp": across if kind == 0 else sibling},
        )

    def x_recv(kind, s):
        target = batch_of((across, sibling, diagonal)[kind], s)
        return remote(
            target,
            target,
            x_send_sem.at[kind, s],
            x_recv_sem.at[kind, s],
            {"mp": across if kind == 0 else sibling},
        )

    others = (across, sibling, diagonal)
    low_device = [{"mp": b} for b in others] + [{"groups": 1 - g, "mp": b} for b in others + (m,)]

    def share_of(b):
        return pl.ds(pl.multiple_of(b * share, 16), share)

    def low_copy(i):
        return remote(
            low_sent.at[0 if i < 3 else 1, share_of((others + others + (m,))[i])],
            low_all.at[g, m],
            low_send_sem.at[i],
            low_recv_sem.at[i],
            low_device[i],
        )

    def low_recv(i):
        target = low_all.at[g if i < 3 else 1 - g, (others + others + (m,))[i]]
        return remote(target, target, low_send_sem.at[i], low_recv_sem.at[i], low_device[i])

    def full_copy(i):
        here = low_full.at[share_of(m)]
        return remote(here, here, full_send_sem.at[i], full_recv_sem.at[i], low_device[i])

    def full_recv(i):
        target = low_full.at[share_of(others[i])]
        return remote(target, target, full_send_sem.at[i], full_recv_sem.at[i], low_device[i])

    local = [
        pltpu.make_async_copy(lengths, small.at[0], local_sem.at[0]),
        pltpu.make_async_copy(holder, small.at[1], local_sem.at[1]),
        pltpu.make_async_copy(place, small.at[2], local_sem.at[2]),
        pltpu.make_async_copy(tok, tok_all.at[m], local_sem.at[3]),
        pltpu.make_async_copy(down.at[:, features(g, 0, helped)], down_all.at[z, 0], local_sem.at[4]),
        pltpu.make_async_copy(
            down.at[:, features(g, helped, helped)], down_all.at[z, 1], local_sem.at[7]
        ),
        pltpu.make_async_copy(weight, weight_here, local_sem.at[5]),
        pltpu.make_async_copy(up, up_all.at[z], local_sem.at[6]),
    ]
    for copy in local:
        copy.start()

    barrier = pltpu.get_barrier_semaphore()
    for device in low_device:
        pl.semaphore_signal(barrier, inc=1, device_id=device, device_id_type=MESH)
    for way in range(2):

        @pl.when(has_next(way))
        def _(way=way):
            pl.semaphore_signal(
                barrier, inc=1, device_id={"req": z + step_of(way)}, device_id_type=MESH
            )

    prompts = lengths.shape[1]
    for copy in local[:3]:
        copy.wait()
    lens = small[0]
    adapter = small[1] * held + small[2]
    row = lax.broadcasted_iota(jnp.int32, (8, prompts), 0)
    prompts_of[0] = jnp.where(row == 0, lens, adapter)

    beside = lax.div(z + peers - 1, peers) + lax.div(2 * peers - 2 - z, peers)
    pl.semaphore_wait(barrier, 7 + beside)

    pl.when(is_end)(end_copy(0).start)
    order = [*range(batches), PIECES, *range(batches, PIECES)]
    for c in order:
        for way in range(2):
            pl.when(has_next(way, c))(z_send(way, 0, c).start)
    prompt_copy = remote(
        prompts_of.at[0],
        prompts_of.at[1],
        prompt_send_sem.at[0],
        prompt_recv_sem.at[0],
        {"groups": 1 - g},
    )
    prompt_copy.start()
    for s in range(SLICES):
        x_copy(0, s).start()
    for s in (1, 0):
        t_copy(s).start()
    for s in range(SLICES):
        x_copy(1, s).start()

    def name_adapters(which):
        table = prompts_of if which < 2 else prompts_end
        lens = table[which % 2, 0:1]
        earlier = lax.broadcasted_iota(jnp.int32, (prompts, prompts), 0) <= lax.broadcasted_iota(
            jnp.int32, (prompts, prompts), 1
        )
        ends = jnp.dot(
            jnp.broadcast_to(lens, (8, prompts)).astype(jnp.float32).astype(jnp.bfloat16),
            earlier.astype(jnp.float32).astype(jnp.bfloat16),
            preferred_element_type=jnp.float32,
        )[0:1].astype(jnp.int32)
        position = lax.broadcasted_iota(jnp.int32, (rows, prompts), 0)
        inside = (position < ends) & (position >= ends - lens)
        named = jnp.where(inside, table[which % 2, 1:2], 0)
        adapter_of[which] = jnp.sum(named, axis=1, keepdims=True)

    name_adapters(0)

    def add_base(b, first=False):
        term = jnp.dot(
            tok_all[b],
            weight_here[pl.ds(pl.multiple_of(b * feats, 128), feats)],
            preferred_element_type=jnp.float32,
        )
        if first:
            base[...] = term
        else:
            base[...] += term

    def member(which, h, part):
        lane = lax.broadcasted_iota(jnp.int32, (1, width), 1)
        return adapter_of[which, part * half : (part + 1) * half, :] == lane // rank + h * held

    def fold(part, turned):
        shape = (2 * rank, width) if turned else (width, 2 * rank)
        one = lax.broadcasted_iota(jnp.int32, shape, 1 if turned else 0)
        two = lax.broadcasted_iota(jnp.int32, shape, 0 if turned else 1)
        return (lax.rem(one, rank) == two - part * rank).astype(jnp.float32).astype(jnp.bfloat16)

    def add_low(which, h, start, count, first=False):
        partial = jnp.zeros((rows, width), jnp.float32)
        for i in range(start // helped, (start + count) // helped):
            if which == 0:
                features_here = tok_all[m, :, features(g, i * helped, helped)]
            elif which == 1:
                features_here = tok_other[i]
            else:
                features_here = tok_end[which - 2]
            partial += lax.dot_general(
                features_here,
                down_all[h, i],
                (((1,), (1,)), ((), ())),
                preferred_element_type=jnp.float32,
            )
        total = jnp.zeros((half, 2 * rank), jnp.float32)
        for part in range(2):
            ours = partial[part * half : (part + 1) * half]
            kept = jnp.where(member(which, h, part), ours, 0.0).astype(jnp.bfloat16)
            total += jnp.dot(kept, fold(part, False), preferred_element_type=jnp.float32)
        if first:
            low_sum[which] = total
        else:
            low_sum[which] += total

    def add_held(which, way, d):
        h = z - step_of(way) * d
        pl.when(has(way, d) & inner(z))(lambda: add_low(which, h, 0, mine))
        pl.when(has(way, d) & is_end)(lambda: add_low(which, h, 0, helped))

    def help_first(i):
        @pl.when(is_helper)
        def _():
            end_recv(i).wait_recv()
            if i == 0:
                end_recv(2).wait_recv()
            name_adapters(2 + i)
            add_low(2 + i, z, helped, helped, first=True)
            for d in range(1, peers - 2):
                add_low(2 + i, z - outward * d, helped, helped)

    def help_last(i):
        @pl.when(is_helper)
        def _():
            add_low(2 + i, z - outward * (peers - 2), helped, helped)
            low_back[0, i] = low_sum[2 + i].astype(jnp.bfloat16)
            back_copy(i).start()

    local[3].wait()
    local[4].wait()
    local[5].wait()
    add_low(0, z, 0, mine, first=True)
    local[6].wait()
    add_base(m, first=True)
    x_slots = {2: 0, 5: 1, 8: 2, 11: 3}
    slot = 0
    for d in range(1, peers):
        for c in order:
            if d == peers - 2 and c == batches:
                help_first(1)
            for way in range(2):
                pass_on(way, d, c, has(way, d, c))
            if c == PIECES:
                continue
            if slot in x_slots:
                x_recv(0, x_slots[slot]).wait_recv()
                x_copy(2, x_slots[slot]).start()
            if slot == 1:
                prompt_copy.wait_recv()
                t_copy(1).wait_recv()

                @pl.when(is_end)
                def _():
                    end_copy(2).start()
                    end_copy(1).start()

            slot += 1
        if d == 1:
            help_first(0)
        if d == peers - 2:
            help_last(0)
            help_last(1)
        if d == 1:
            name_adapters(1)
            t_copy(0).wait_recv()
            add_low(1, z, 0, mine, first=True)
            for s in range(SLICES):
                x_recv(1, s).wait_recv()
            add_base(sibling)
        for way in range(2):
            for which in range(2):
                add_held(which, way, d)

    @pl.when(is_end)
    def _():
        for i in range(2):
            back_recv(i).wait_recv()
            low_sum[i] += low_back[1, i].astype(jnp.float32)

    low_sent[...] = low_sum[0:2].astype(jnp.bfloat16)
    for i in range(7):
        low_copy(i).start()
    low_all[g, m] = low_sent[0, share_of(m)]
    add_base(across)
    for i in range(7):
        low_recv(i).wait_recv()
    low = low_all[0, 0].astype(jnp.float32)
    for i in range(1, 8):
        low += low_all[i // 4, i % 4].astype(jnp.float32)
    low_full[share_of(m)] = low.astype(jnp.bfloat16)
    for i in range(3):
        full_copy(i).start()
    for s in range(SLICES):
        x_recv(2, s).wait_recv()
    add_base(diagonal)
    local[7].wait()
    for d in range(1, peers):
        for way in range(2):
            pl.when(has(way, d))(y_copy(way, d, 1 - g).wait_recv)
    for i in range(3):
        full_recv(i).wait_recv()
    low = low_full[...]
    for part in range(2):
        spread = jnp.dot(low, fold(part, True), preferred_element_type=jnp.float32)
        term = jnp.zeros((half, cols), jnp.float32)
        for h in range(peers):
            kept = jnp.where(member(0, h, part), spread, 0.0).astype(jnp.bfloat16)
            term += jnp.dot(kept, up_all[h], preferred_element_type=jnp.float32)
        term = term.astype(jnp.bfloat16).astype(jnp.float32)
        here = pl.ds(part * half, half)
        out[here, :] = (base[here, :] + 0.5 * term).astype(jnp.bfloat16)

    for i in range(3):
        full_copy(i).wait_send()
        pl.when(is_end)(end_copy(i).wait_send)
    for i in range(2):
        pl.when(is_helper)(back_copy(i).wait_send)
    prompt_copy.wait_send()
    for s in range(2):
        t_copy(s).wait_send()
    for s in range(SLICES):
        for kind in range(3):
            x_copy(kind, s).wait_send()
    for i in range(7):
        low_copy(i).wait_send()
    for way in range(2):
        for c in range(PIECES + 1):
            for d in range(peers - 1):
                sent = has_next(way, c) if d == 0 else has_next(way, c) & has(way, d, c)
                pl.when(sent)(z_send(way, d, c).wait_send)
        for d in range(1, peers):
            pl.when(has(way, d))(y_copy(way, d, g).wait_send)


def grouped_update(token_rows, slot_ids, down_factor_sets, up_sets, reduce_fn):
    count = token_rows.shape[0] * token_rows.shape[1]
    flat_rows = token_rows.reshape(count, token_rows.shape[2])
    flat_ids = slot_ids.reshape(count)
    held = down_factor_sets.shape[0]
    blocks = (count + 127) // 128 + held
    grouped = blocks * 128
    valid = flat_ids >= 0
    member = (flat_ids[:, None] == jnp.arange(held, dtype=jnp.int32)[None, :]).astype(jnp.int32)
    group_sizes = jnp.sum(member, axis=0)
    padded = (group_sizes + 127) // 128 * 128
    group_end = jnp.cumsum(padded)
    group_start = group_end - padded
    within = jnp.sum(jnp.cumsum(member, axis=0) * member, axis=1) - 1
    target = jnp.where(valid, jnp.sum(member * group_start[None, :], axis=1) + within, grouped)
    source = (
        jnp.zeros((grouped,), jnp.int32)
        .at[target]
        .set(jnp.arange(count, dtype=jnp.int32), mode="drop")
    )
    filled = jnp.zeros((grouped,), jnp.bool_).at[target].set(True, mode="drop")
    grouped_rows = jnp.where(filled[:, None], flat_rows[source], jnp.zeros((), jnp.bfloat16))
    grouped_rows = grouped_rows.reshape(blocks, 128, flat_rows.shape[1])
    block_first = jnp.arange(blocks, dtype=jnp.int32) * 128
    block_adapter = jnp.minimum(
        jnp.sum((block_first[:, None] >= group_end[None, :]).astype(jnp.int32), axis=1), held - 1
    )
    partial_value = jnp.einsum(
        "bkf,bfr->bkr",
        grouped_rows,
        down_factor_sets[block_adapter],
        preferred_element_type=jnp.float32,
    )
    reduced_rank_output = reduce_fn(partial_value).astype(jnp.bfloat16)
    term = jnp.einsum(
        "bkr,brc->bkc",
        reduced_rank_output,
        up_sets[block_adapter],
        preferred_element_type=jnp.float32,
    )
    term = term.astype(jnp.bfloat16).reshape(grouped, up_sets.shape[2])
    picked = jnp.where(
        valid[:, None], term[jnp.minimum(target, grouped - 1)], jnp.zeros((), jnp.bfloat16)
    )
    return picked.reshape(token_rows.shape[0], token_rows.shape[1], up_sets.shape[2])


def body(
    tokens,
    lengths,
    adapter_holder_index,
    adapter_place_index,
    value_weight,
    adapter_down_weight,
    adapter_up_weight,
):
    tok_rows = tokens.shape[0]
    peers = lax.axis_size("req")
    request_cap = max(2, REQ_DEV // peers + 1)
    slots = request_cap * LMAX
    lengths_row = lengths[0]
    prompt_ends = jnp.cumsum(lengths_row)
    prompt_starts = prompt_ends - lengths_row
    owners = adapter_holder_index[:, 0]
    request_index = jnp.arange(REQ_DEV, dtype=jnp.int32)
    earlier = (owners[None, :] == owners[:, None]) & (
        request_index[None, :] < request_index[:, None]
    )
    rank_among = jnp.sum(earlier.astype(jnp.int32), axis=1)
    matches = (owners[None, None, :] == jnp.arange(peers, dtype=jnp.int32)[:, None, None]) & (
        rank_among[None, None, :] == jnp.arange(request_cap, dtype=jnp.int32)[None, :, None]
    )
    present = jnp.any(matches, axis=2)
    chosen = jnp.sum(matches.astype(jnp.int32) * request_index[None, None, :], axis=2)
    offsets = jnp.arange(LMAX, dtype=jnp.int32)
    live = present[:, :, None] & (offsets[None, None, :] < lengths_row[chosen][:, :, None])
    source_row = jnp.where(
        live, prompt_starts[chosen][:, :, None] + offsets[None, None, :], 0
    ).reshape(peers, slots)
    slot_ids = jnp.where(live, adapter_place_index[chosen][:, :, None], -1).reshape(peers, slots, 1)
    send_rows = jnp.where(
        live.reshape(peers, slots)[:, :, None], tokens[source_row], jnp.zeros((), jnp.bfloat16)
    )
    base_output = jnp.dot(
        lax.all_gather(tokens, "mp", axis=1, tiled=True),
        value_weight,
        preferred_element_type=jnp.float32,
    )
    down_factor_sets = jnp.transpose(adapter_down_weight, (1, 0, 2))

    def mp_total(partial_value):
        return lax.psum(partial_value, "mp")

    adapter_update = grouped_update(
        lax.all_to_all(send_rows, "req", split_axis=0, concat_axis=0, tiled=True),
        lax.all_to_all(slot_ids, "req", split_axis=0, concat_axis=0, tiled=True),
        down_factor_sets,
        adapter_up_weight,
        mp_total,
    )
    value_output = lax.all_to_all(adapter_update, "req", split_axis=0, concat_axis=0, tiled=True)
    position = jnp.arange(tok_rows, dtype=jnp.int32)
    request_of = jnp.sum((position[:, None] >= prompt_ends[None, :]).astype(jnp.int32), axis=1)
    flat_index = (
        owners[request_of] * slots
        + rank_among[request_of] * LMAX
        + position
        - prompt_starts[request_of]
    )
    gathered_terms = value_output.reshape(peers * slots, value_output.shape[2])[flat_index]
    return (base_output + 0.5 * gathered_terms.astype(jnp.float32)).astype(jnp.bfloat16)


def gather_body(mesh, *args):
    tokens, lengths, holder, place, value_weight, down, up = args
    peers, mp = mesh.shape["req"], mesh.shape["mp"]
    rows, feats = tokens.shape
    held, rank, cols = up.shape
    prompts = lengths.shape[1]
    down_rows = jnp.transpose(down, (1, 2, 0)).reshape(held * rank, feats)
    up_rows = up.reshape(held * rank, cols)
    anywhere = pl.BlockSpec(memory_space=pltpu.HBM)
    vmem = pl.BlockSpec(memory_space=pltpu.VMEM)
    dma = pltpu.SemaphoreType.DMA
    hops = max(peers - 1, 1)
    return pl.pallas_call(
        functools.partial(adapter_kernel, peers, held, rank),
        out_shape=jax.ShapeDtypeStruct((rows, cols), jnp.bfloat16),
        in_specs=[anywhere] * 7,
        out_specs=vmem,
        scratch_shapes=[
            pltpu.VMEM((mp, rows, feats), jnp.bfloat16),
            pltpu.VMEM((2, rows, feats // 4), jnp.bfloat16),
            pltpu.VMEM(value_weight.shape, jnp.bfloat16),
            pltpu.VMEM((peers, 2, held * rank, feats // 4), jnp.bfloat16),
            pltpu.VMEM((peers, held * rank, cols), jnp.bfloat16),
            pltpu.VMEM((2, mp, rows // 8, 2 * rank), jnp.bfloat16),
            pltpu.VMEM((2, rows // 2, 2 * rank), jnp.bfloat16),
            pltpu.VMEM((rows // 2, 2 * rank), jnp.bfloat16),
            pltpu.VMEM((2, 2, rows // 2, 2 * rank), jnp.bfloat16),
            pltpu.VMEM((2, rows, feats // 4), jnp.bfloat16),
            pltpu.VMEM((2, 8, prompts), jnp.int32),
            pltpu.VMEM((rows, cols), jnp.float32),
            pltpu.VMEM((4, rows // 2, 2 * rank), jnp.float32),
            pltpu.VMEM((3, 1, prompts), jnp.int32),
            pltpu.VMEM((2, 8, prompts), jnp.int32),
            pltpu.VMEM((4, rows, 1), jnp.int32),
            dma((8,)),
            dma((1,)),
            dma((1,)),
            dma((2,)),
            dma((2,)),
            dma((2, hops, PIECES + 1)),
            dma((2, hops, PIECES + 1)),
            dma((2, hops)),
            dma((2, hops)),
            dma((3, SLICES)),
            dma((3, SLICES)),
            dma((7,)),
            dma((7,)),
            dma((3,)),
            dma((3,)),
            dma((3,)),
            dma((3,)),
            dma((2,)),
            dma((2,)),
        ],
        compiler_params=pltpu.CompilerParams(
            collective_id=0, has_side_effects=True, vmem_limit_bytes=63 << 20
        ),
        cost_estimate=pl.CostEstimate(
            flops=2 * rows * feats * (mp * cols + peers * held * rank),
            bytes_accessed=2 * (rows * feats + value_weight.size + down.size + up.size),
            transcendentals=0,
        ),
    )(
        tokens,
        lengths,
        holder.reshape(1, -1),
        place.reshape(1, -1),
        value_weight,
        down_rows,
        up_rows,
    )


def solution(mesh):
    placed = (
        P(("groups", "req"), "mp"),
        P(("groups", "req"), None),
        P(("groups", "req"), None),
        P(("groups", "req")),
        P(None, "mp"),
        P("mp", "req", None),
        P("req", None, "mp"),
    )

    def whole(*args):
        peers = mesh.shape["req"]
        moved = 2 * (args[5].size // mesh.shape["mp"] + args[6].size // mesh.shape["mp"])
        fits = moved <= GATHER_BYTES and peers == 4
        if fits and mesh.shape["mp"] == 4 and mesh.shape["groups"] == 2:
            part = functools.partial(gather_body, mesh)
        else:
            part = body
        return jax.shard_map(
            part, mesh=mesh, in_specs=placed, out_specs=P(("groups", "req"), "mp"), check_vma=False
        )(*args)

    return whole
```
